32 devices in a mesh: groups: 2 (over y), seq: 8 (over z, x), head: 2 (over core).
Axes of the slice: x: 2, y: 2, z: 4, core: 2. Of those that a mesh axis runs over, the one named last changes fastest.
Arguments:
- big_queries: bfloat16 [512, 4096], P(('groups', 'seq'), 'head'), parts along dimension 0, may hold values from -160 to 160
- big_keys: bfloat16 [512, 4096], P(('groups', 'seq'), 'head'), parts along dimension 0, may hold values from -8 to 8
- big_values: bfloat16 [512, 4096], P(('groups', 'seq'), 'head'), parts along dimension 0, may hold values from -6 to 6
- small_queries: bfloat16 [512, 1024], P(('groups', 'seq', 'head')), parts along dimension 0, may hold values from -160 to 160
- small_keys: bfloat16 [512, 1024], P(('groups', 'seq', 'head')), parts along dimension 0, may hold values from -8 to 8
- small_values: bfloat16 [512, 1024], P(('groups', 'seq', 'head')), parts along dimension 0, may hold values from -6 to 6
- big_readout: bfloat16 [4096, 64], P('head'), may hold values from -0.75 to 0.75
- small_readout: bfloat16 [1024, 64], replicated, may hold values from -1.5 to 1.5
- guidance: float32 [2], P('groups'), parts along dimension 0, may hold values from 1 to 4
Outputs:
- guided: float32 [256, 128], P(('groups', 'seq')), parts along dimension 0
The draws below stay inside these ranges and needn't reach their ends.
There are 2 independent parts, one for each index of `groups`. The reference program is written for one: setup_inputs(seed, part) draws one part's arguments, and reference() takes and returns one part's arrays. A program takes and returns all parts, laid end to end along the dimension named above; an argument that names none is the same for every part. Nothing has to cross between parts.
All inputs are finite; a program needn't handle non-finite values.
Results may differ from the reference program's by a relative error of at most 0.0035.
Values may be sent and summed in bfloat16 or wider, within the bound.
No kernel may reach another device: no remote copies, remote signals or barrier semaphores. Data moves between devices by JAX's collectives and lax.ppermute only.
A program may use at most 64 MiB of HBM per device.

```python
import math
import jax
import jax.numpy as jnp
from jax import lax

DH = 128
HB = 32
HS = 8
LAT = 64
TOKENS = 256


def paired(key, heads, salt):
    folded = jax.random.fold_in(key, salt)
    query_seed, key_seed = jax.random.split(folded, 2)
    extent = (TOKENS, heads, DH)
    query_draw = jnp.clip(1.41 * jax.random.normal(query_seed, extent, jnp.float32), -8.0, 8.0)
    key_draw = jnp.clip(1.41 * jax.random.normal(key_seed, extent, jnp.float32), -8.0, 8.0)
    return (query_draw.reshape(TOKENS, heads * DH), key_draw.reshape(TOKENS, heads * DH))


def draw_big_queries(key, part):
    return paired(key, HB, 101)[0].astype(jnp.bfloat16)


def draw_big_keys(key, part):
    return paired(key, HB, 101)[1].astype(jnp.bfloat16)


def draw_small_queries(key, part):
    return paired(key, HS, 202)[0].astype(jnp.bfloat16)


def draw_small_keys(key, part):
    return paired(key, HS, 202)[1].astype(jnp.bfloat16)


def shard_levels(key, shape, cuts, least, top_value):
    def one(dim, shards_of):
        draws = jax.random.uniform(jax.random.fold_in(jax.random.fold_in(key, 6), dim), (shards_of,), jnp.float32, least / len(cuts), top_value / len(cuts))
        return jnp.repeat(jnp.exp(draws), shape[dim] // shards_of).reshape((-1,) + (1,) * (len(shape) - dim - 1))

    factor_of = one(*cuts[0])
    for cut in cuts[1:]:
        factor_of = factor_of * one(*cut)
    return factor_of


def gaussian(stream_key, dims, scale, limit, pieces=(), held_as=jnp.bfloat16):
    array = scale * jax.random.normal(stream_key, dims, jnp.float32)
    if pieces:
        array = array * shard_levels(stream_key, dims, pieces, -0.22, 0.18)
    return jnp.clip(array, -limit, limit).astype(held_as)


def setup_inputs(seed: int = 0, part: int = 0) -> dict:
    splits = jax.random.split(jax.random.key(seed), 10)
    part_keys = jax.random.split(jax.random.fold_in(splits[9], part), 10)
    big_queries = draw_big_queries(jax.random.fold_in(jax.random.fold_in(splits[9], part), 71), part)
    big_keys = draw_big_keys(jax.random.fold_in(jax.random.fold_in(splits[9], part), 71), part)
    big_values = gaussian(part_keys[2], (TOKENS, HB * DH), 1.0, 6.0, ((0, 8), (1, 2)))
    small_queries = draw_small_queries(jax.random.fold_in(jax.random.fold_in(splits[9], part), 71), part)
    small_keys = draw_small_keys(jax.random.fold_in(jax.random.fold_in(splits[9], part), 71), part)
    small_values = gaussian(part_keys[5], (TOKENS, HS * DH), 1.0, 6.0, ((0, 16),))
    big_readout = gaussian(splits[6], (HB * DH, LAT), (max(HB * DH // 64, 1)) ** -0.5, 0.75, ((0, 2),))
    small_readout = gaussian(splits[7], (HS * DH, LAT), (max(HS * DH // 64, 1)) ** -0.5, 1.5)
    guidance = jnp.clip(jax.random.uniform(part_keys[8], (1,), jnp.float32, 1.0, 4.0), 1.0, 4.0)
    return dict(big_queries=big_queries, big_keys=big_keys, big_values=big_values, small_queries=small_queries, small_keys=small_keys, small_values=small_values, big_readout=big_readout, small_readout=small_readout, guidance=guidance)


def attend_head(operands):
    query_head, key_head, value_head = operands
    scores = jnp.dot(query_head, key_head.T, preferred_element_type=jnp.float32) * (1.0 / math.sqrt(DH))
    row_max = lax.optimization_barrier(jnp.max(scores, axis=1, keepdims=True))
    probs = jnp.exp(scores - row_max)
    totals = lax.optimization_barrier(jnp.sum(probs, axis=1, keepdims=True))
    weights = probs.astype(jnp.bfloat16)
    attended = jnp.dot(weights, value_head, preferred_element_type=jnp.float32) / totals
    return attended.astype(jnp.bfloat16)

def split_model(matrix, heads):
    return jnp.transpose(matrix.reshape(TOKENS, heads, DH), (1, 0, 2))

def run_model(query_all, key_all, value_all, heads):
    outputs = lax.map(attend_head, (split_model(query_all, heads), split_model(key_all, heads), split_model(value_all, heads)))
    return jnp.transpose(outputs, (1, 0, 2)).reshape(TOKENS, heads * DH)

def reference(big_queries, big_keys, big_values, small_queries, small_keys, small_values, big_readout, small_readout, guidance):
    big_attention = run_model(big_queries, big_keys, big_values, HB)
    small_attention = run_model(small_queries, small_keys, small_values, HS)
    big_latent = jnp.dot(big_attention, big_readout, preferred_element_type=jnp.float32)
    small_latent = jnp.dot(small_attention, small_readout, preferred_element_type=jnp.float32)
    blended = big_latent + guidance[0] * (big_latent - small_latent)
    return blended.reshape(TOKENS // 2, 2 * LAT)
```

```python
import functools
import math

import jax
import jax.numpy as jnp
from jax import lax
from jax.experimental import pallas as pl
from jax.experimental.pallas import tpu as pltpu
from jax.sharding import PartitionSpec as P

DH = 128
BF16 = jnp.bfloat16
F32 = jnp.float32
VMEM = pl.BlockSpec(memory_space=pltpu.VMEM)
SMEM = pl.BlockSpec(memory_space=pltpu.SMEM)
NT = (((1,), (1,)), ((), ()))


def row_layout(group, tokens, small_tokens):
    rows = {}
    at = 0
    for name, count in (
        ("q", group * tokens),
        ("k", group * tokens),
        ("vr", tokens),
        ("sq", small_tokens),
        ("sk", small_tokens),
        ("svr", small_tokens),
    ):
        rows[name] = at
        at += count
    rows["all"] = at
    return rows


def pack_kernel(n, group, bq, bk, bv, sq, sk, sv, br, sr, *outs):
    tokens, small_tokens = bq.shape[0], sq.shape[0]
    lat = br.shape[0]
    rows = row_layout(group, tokens, small_tokens)
    me = lax.axis_index("seq")
    for k in range(n):
        out = outs[k]
        dest = jnp.bitwise_xor(me, k)
        values = []
        for g in range(group):
            cols = pl.ds(pl.multiple_of((dest * group + g) * DH, DH), DH)
            out[pl.ds(rows["q"] + g * tokens, tokens), :] = bq[:, cols]
            out[pl.ds(rows["k"] + g * tokens, tokens), :] = bk[:, cols]
            values.append(
                lax.dot_general(bv[:, cols], br[:, cols], NT, preferred_element_type=F32)
            )
        out[pl.ds(rows["vr"], tokens), :] = jnp.concatenate(values, axis=1).astype(BF16)
        cols = pl.ds(pl.multiple_of(dest * DH, DH), DH)
        out[pl.ds(rows["sq"], small_tokens), :] = sq[:, cols]
        out[pl.ds(rows["sk"], small_tokens), :] = sk[:, cols]
        value = lax.dot_general(sv[:, cols], sr[:, cols], NT, preferred_element_type=F32)
        value = jnp.concatenate([value, jnp.zeros((small_tokens, DH - lat), F32)], axis=1)
        out[pl.ds(rows["svr"], small_tokens), :] = value.astype(BF16)


def gather_small_kernel(n, first, count, *refs):
    out = refs[n]
    for k in range(n):
        out[pl.ds(k * count, count), :] = refs[k][pl.ds(first, count), :]


def softmax_times(queries, keys, values):
    scores = lax.dot_general(queries, keys, NT, preferred_element_type=F32)
    scores = scores * (1.0 / math.sqrt(DH))
    probs = jnp.exp(scores - jnp.max(scores, axis=1, keepdims=True))
    totals = jnp.sum(probs, axis=1, keepdims=True)
    out = jnp.dot(probs.astype(BF16), values, preferred_element_type=F32)
    return out / totals


def big_kernel(n, group, tokens, lat, rows, *refs):
    blocks, out = refs[:n], refs[n]
    read = lambda first: jnp.concatenate([b[pl.ds(first, tokens), :] for b in blocks], axis=0)
    values = read(rows["vr"])
    total = None
    for g in range(group):
        part = softmax_times(
            read(rows["q"] + g * tokens),
            read(rows["k"] + g * tokens),
            values[:, g * lat : (g + 1) * lat],
        )
        total = part if total is None else total + part
    out[:, :] = total


def small_kernel(n, tokens, small_tokens, lat, rows, copies, *refs):
    blocks = refs[:n]
    own_kv, other_kv, big, guidance, out, latent = refs[n:]
    me, core = lax.axis_index("seq"), lax.axis_index("head")
    weight = guidance[0]
    queries = jnp.concatenate([b[pl.ds(rows["sq"], small_tokens), :] for b in blocks], axis=0)
    pick = lambda kv, first: [
        kv[pl.ds(k * 2 * small_tokens + first, small_tokens), :] for k in range(n)
    ]
    keys = jnp.concatenate(pick(own_kv, 0) + pick(other_kv, 0), axis=0)
    values = jnp.concatenate(
        pick(own_kv, small_tokens) + pick(other_kv, small_tokens), axis=0
    )
    small = softmax_times(queries, keys, values[:, :lat])
    latent[:, :lat] = (1.0 + weight) * big[:, :]
    for k in range(n):
        at = pl.multiple_of(k * tokens + core * small_tokens, small_tokens)
        here = pl.ds(at, small_tokens)
        latent[here, :lat] = (
            latent[here, :lat] - weight * small[k * small_tokens : (k + 1) * small_tokens, :]
        )
    for k in range(n):
        even = latent[pl.ds(k * tokens, tokens // 2, stride=2), :lat]
        odd = latent[pl.ds(k * tokens + 1, tokens // 2, stride=2), :lat]
        block = jnp.concatenate([even, odd], axis=1).astype(out.dtype)
        dest = jnp.bitwise_xor(me, k)
        for c in range(copies):
            out[dest * copies + c] = block


def sum_kernel(x, out):
    total = x[0].astype(F32)
    for i in range(1, x.shape[0]):
        total = total + x[i].astype(F32)
    out[:, :] = total


def call(kernel, out_shape, operands, specs=None, scratch=(), cost=None):
    single = not isinstance(out_shape, (list, tuple))
    return pl.pallas_call(
        kernel,
        out_shape=out_shape,
        in_specs=specs if specs is not None else [VMEM] * len(operands),
        out_specs=VMEM if single else [VMEM] * len(out_shape),
        scratch_shapes=list(scratch),
        cost_estimate=cost,
        compiler_params=pltpu.CompilerParams(vmem_limit_bytes=32 * 1024 * 1024),
    )(*operands)


def exchange_shards(bq, bk, bv, sq, sk, sv, br, sr, guidance):
    n, cores = lax.axis_size("seq"), lax.axis_size("head")
    tokens, small_tokens = bq.shape[0], sq.shape[0]
    group = bq.shape[1] // DH // n
    lat = br.shape[1]
    rows = row_layout(group, tokens, small_tokens)
    block = jax.ShapeDtypeStruct((rows["all"], DH), BF16)
    sent = call(
        functools.partial(pack_kernel, n, group),
        [block] * n,
        (bq, bk, bv, sq, sk, sv, br.T, sr.T),
    )
    blocks = [sent[0]] + [None] * (n - 1)
    for k in range(n - 1, 0, -1):
        blocks[k] = lax.ppermute(sent[k], "seq", [(j, j ^ k) for j in range(n)])
    own_kv = call(
        functools.partial(gather_small_kernel, n, rows["sk"], 2 * small_tokens),
        jax.ShapeDtypeStruct((n * 2 * small_tokens, DH), BF16),
        blocks,
    )
    other_kv = lax.ppermute(own_kv, "head", [(c, c ^ 1) for c in range(cores)])
    big = call(
        functools.partial(big_kernel, n, group, tokens, lat, rows),
        jax.ShapeDtypeStruct((n * tokens, lat), F32),
        blocks,
        cost=pl.CostEstimate(flops=10**9, bytes_accessed=10**6, transcendentals=10**5),
    )
    partial = call(
        functools.partial(small_kernel, n, tokens, small_tokens, lat, rows, cores),
        jax.ShapeDtypeStruct((n * cores, tokens // 2, 2 * lat), BF16),
        (*blocks, own_kv, other_kv, big, guidance),
        specs=[VMEM] * (n + 3) + [SMEM],
        scratch=[pltpu.VMEM((n * tokens, DH), F32)],
    )
    terms = lax.all_to_all(partial, ("seq", "head"), split_axis=0, concat_axis=0, tiled=True)
    return call(
        sum_kernel, jax.ShapeDtypeStruct((tokens // 2, 2 * lat), F32), (terms,)
    )


def fits_exchange(mesh, bq, sq, br):
    groups, n, cores = mesh.shape["groups"], mesh.shape["seq"], mesh.shape["head"]
    tokens = bq.shape[0] // (groups * n)
    small_tokens = sq.shape[0] // (groups * n * cores)
    big_heads, small_heads = bq.shape[1] // DH // cores, sq.shape[1] // DH
    lat = br.shape[1]
    return (
        cores == 2
        and n & (n - 1) == 0
        and small_heads == n
        and big_heads % n == 0
        and big_heads // n * lat == DH
        and 2 * lat == DH
        and tokens % 32 == 0
        and small_tokens % 16 == 0
        and n * tokens <= 1024
    )


def split_heads(matrix, blocks, parts):
    rows_here, columns = matrix.shape
    shaped = matrix.reshape(blocks, rows_here // blocks, parts, columns // parts)
    shaped = jnp.transpose(shaped, (0, 2, 1, 3))
    return shaped.reshape(blocks * parts, rows_here // blocks, columns // parts)


def copy_heads(matrix, blocks, parts):
    rows_here, columns = matrix.shape
    shaped = jnp.transpose(matrix.reshape(rows_here, parts, columns // parts), (1, 0, 2))
    shaped = jnp.broadcast_to(shaped[None], (blocks, parts, rows_here, columns // parts))
    return shaped.reshape(blocks * parts, rows_here, columns // parts)


def join_heads(stacked, blocks, parts):
    pieces, rows_here, columns = stacked.shape
    shaped = stacked.reshape(blocks, parts, rows_here, columns)
    shaped = jnp.transpose(shaped, (0, 2, 1, 3))
    return shaped.reshape(blocks * rows_here, parts * columns)


def attend(query_rows, key_rows, value_rows):
    query_count = query_rows.shape[0]
    heads_here = query_rows.shape[1] // DH
    key_count = key_rows.shape[0]
    block_height = math.gcd(query_count, 256)
    block_count = query_count // block_height
    query_blocks = query_rows.reshape(block_count, block_height, heads_here, DH)
    key_split = key_rows.reshape(key_count, heads_here, DH)
    value_split = value_rows.reshape(key_count, heads_here, DH)
    score_scale = 1.0 / math.sqrt(DH)

    def one_block(query_block):
        scores = (
            jnp.einsum("qgd,kgd->gqk", query_block, key_split, preferred_element_type=F32)
            * score_scale
        )
        row_max = jnp.max(scores, axis=2, keepdims=True)
        probs = jnp.exp(scores - row_max)
        totals = jnp.sum(probs, axis=2, keepdims=True)
        weights = probs.astype(BF16)
        accumulated = jnp.einsum(
            "gqk,kgd->gqd", weights, value_split, preferred_element_type=F32
        )
        attended = accumulated / totals
        attended = jnp.transpose(attended, (1, 0, 2)).reshape(block_height, heads_here * DH)
        return attended.astype(BF16)

    outputs = lax.map(one_block, query_blocks)
    return outputs.reshape(query_count, heads_here * DH)


def seq_exchange(stacked, split, concat):
    return lax.all_to_all(stacked, "seq", split_axis=split, concat_axis=concat, tiled=True)


def run_model(queries, keys, values, shared):
    seq_count = lax.axis_size("seq")
    heads = queries.shape[1] // DH
    blocks = max(seq_count // heads, 1)
    parts = heads // max(heads // seq_count, 1)
    query_rows = seq_exchange(split_heads(queries, blocks, parts), 0, 1)[0]
    key_rows = seq_exchange(copy_heads(keys, blocks, parts), 0, 1)[0]
    value_rows = seq_exchange(copy_heads(values, blocks, parts), 0, 1)[0]
    if shared:
        key_rows = lax.all_gather(key_rows, "head", axis=0, tiled=True)
        value_rows = lax.all_gather(value_rows, "head", axis=0, tiled=True)
    out = attend(query_rows, key_rows, value_rows)
    return join_heads(seq_exchange(out[None], 1, 0), blocks, parts)


def general_shards(bq, bk, bv, sq, sk, sv, br, sr, guidance):
    big_attention = run_model(bq, bk, bv, False)
    big_partial = jnp.dot(big_attention, br, preferred_element_type=F32)
    small_attention = run_model(sq, sk, sv, True)
    small_latent = jnp.dot(small_attention, sr, preferred_element_type=F32)
    weight_value = guidance[0]
    core_index = lax.axis_index("head")
    placed = lax.dynamic_update_slice(
        jnp.zeros_like(big_partial),
        small_latent,
        (core_index * small_latent.shape[0], jnp.zeros((), jnp.int32)),
    )
    blended = lax.psum((1.0 + weight_value) * big_partial - weight_value * placed, "head")
    return blended.reshape(blended.shape[0] // 2, 2 * blended.shape[1])


def solution(mesh):
    placed = (
        P(("groups", "seq"), "head"),
        P(("groups", "seq"), "head"),
        P(("groups", "seq"), "head"),
        P(("groups", "seq", "head"), None),
        P(("groups", "seq", "head"), None),
        P(("groups", "seq", "head"), None),
        P("head", None),
        P(),
        P("groups"),
    )

    def whole(*arrays):
        fits = fits_exchange(mesh, arrays[0], arrays[3], arrays[6])
        return jax.shard_map(
            exchange_shards if fits else general_shards,
            mesh=mesh,
            in_specs=placed,
            out_specs=P(("groups", "seq"), None),
            check_vma=False,
        )(*arrays)

    return whole
```

```python
import functools
import math

import jax
import jax.numpy as jnp
from jax import lax
from jax.experimental import pallas as pl
from jax.experimental.pallas import tpu as pltpu
from jax.sharding import PartitionSpec as P

DH = 128
BF16 = jnp.bfloat16
F32 = jnp.float32
VMEM = pl.BlockSpec(memory_space=pltpu.VMEM)
SMEM = pl.BlockSpec(memory_space=pltpu.SMEM)
NT = (((1,), (1,)), ((), ()))


def row_layout(group, tokens, small_tokens):
    rows = {}
    at = 0
    for name, count in (
        ("q", group * tokens),
        ("k", group * tokens),
        ("vr", tokens),
        ("sq", small_tokens),
        ("sk", small_tokens),
        ("svr", small_tokens),
    ):
        rows[name] = at
        at += count
    rows["all"] = at
    return rows


def pack_kernel(n, group, *refs):
    sources, outs, held, done = refs[:8], refs[8 : 8 + n], refs[8 + n : 16 + n], refs[16 + n]
    copies = [pltpu.make_async_copy(sources[i], held[i], done.at[i]) for i in range(8)]
    for copy in copies:
        copy.start()
    for copy in copies:
        copy.wait()
    bq, bk, bv, sq, sk, sv, br, sr = held
    tokens, small_tokens = bq.shape[0], sq.shape[0]
    lat = br.shape[0]
    rows = row_layout(group, tokens, small_tokens)
    me = lax.axis_index("seq")
    for k in range(n):
        out = outs[k]
        dest = jnp.bitwise_xor(me, k)
        values = []
        for g in range(group):
            cols = pl.ds(pl.multiple_of((dest * group + g) * DH, DH), DH)
            out[pl.ds(rows["q"] + g * tokens, tokens), :] = bq[:, cols]
            out[pl.ds(rows["k"] + g * tokens, tokens), :] = bk[:, cols]
            values.append(
                lax.dot_general(bv[:, cols], br[:, cols], NT, preferred_element_type=F32)
            )
        out[pl.ds(rows["vr"], tokens), :] = jnp.concatenate(values, axis=1).astype(BF16)
        cols = pl.ds(pl.multiple_of(dest * DH, DH), DH)
        out[pl.ds(rows["sq"], small_tokens), :] = sq[:, cols]
        out[pl.ds(rows["sk"], small_tokens), :] = sk[:, cols]
        value = lax.dot_general(sv[:, cols], sr[:, cols], NT, preferred_element_type=F32)
        value = jnp.concatenate([value, jnp.zeros((small_tokens, DH - lat), F32)], axis=1)
        out[pl.ds(rows["svr"], small_tokens), :] = value.astype(BF16)


def hop_order(n):
    return [0] + list(range(n - 1, 0, -1))


def gather_small_kernel(n, first, count, *refs):
    out = refs[n]
    for k in range(n):
        out[pl.ds(k * count, count), :] = refs[k][pl.ds(first, count), :]


def softmax_times(queries, keys, values):
    scores = lax.dot_general(queries, keys, NT, preferred_element_type=F32)
    scores = scores * (1.0 / math.sqrt(DH))
    probs = jnp.exp(scores - jnp.max(scores, axis=1, keepdims=True))
    totals = jnp.sum(probs, axis=1, keepdims=True)
    out = jnp.dot(probs.astype(BF16), values, preferred_element_type=F32)
    return out / totals


def big_kernel(n, group, tokens, lat, rows, *refs):
    blocks, out = refs[:n], refs[n]
    read = lambda first: jnp.concatenate([b[pl.ds(first, tokens), :] for b in blocks], axis=0)
    values = read(rows["vr"])
    total = None
    for g in range(group):
        part = softmax_times(
            read(rows["q"] + g * tokens),
            read(rows["k"] + g * tokens),
            values[:, g * lat : (g + 1) * lat],
        )
        total = part if total is None else total + part
    out[:, :] = total


def small_kernel(n, tokens, small_tokens, lat, rows, copies, *refs):
    blocks = refs[:n]
    own_kv, other_kv, big, guidance, out, latent = refs[n:]
    me, core = lax.axis_index("seq"), lax.axis_index("head")
    weight = guidance[0]
    queries = jnp.concatenate([b[pl.ds(rows["sq"], small_tokens), :] for b in blocks], axis=0)
    pick = lambda kv, first: [
        kv[pl.ds(k * 2 * small_tokens + first, small_tokens), :] for k in range(n)
    ]
    keys = jnp.concatenate(pick(own_kv, 0) + pick(other_kv, 0), axis=0)
    values = jnp.concatenate(
        pick(own_kv, small_tokens) + pick(other_kv, small_tokens), axis=0
    )
    small = softmax_times(queries, keys, values[:, :lat])
    latent[:, :lat] = (1.0 + weight) * big[:, :]
    for k in range(n):
        at = pl.multiple_of(k * tokens + core * small_tokens, small_tokens)
        here = pl.ds(at, small_tokens)
        latent[here, :lat] = (
            latent[here, :lat] - weight * small[k * small_tokens : (k + 1) * small_tokens, :]
        )
    for k in range(n):
        even = latent[pl.ds(k * tokens, tokens // 2, stride=2), :lat]
        odd = latent[pl.ds(k * tokens + 1, tokens // 2, stride=2), :lat]
        block = jnp.concatenate([even, odd], axis=1).astype(out.dtype)
        dest = jnp.bitwise_xor(me, hop_order(n)[k])
        for c in range(copies):
            out[dest * copies + c] = block


def sum_kernel(x, out):
    total = x[0].astype(F32)
    for i in range(1, x.shape[0]):
        total = total + x[i].astype(F32)
    out[:, :] = total


def call(kernel, out_shape, operands, specs=None, scratch=(), cost=None, vmem=16):
    single = not isinstance(out_shape, (list, tuple))
    return pl.pallas_call(
        kernel,
        out_shape=out_shape,
        in_specs=specs if specs is not None else [VMEM] * len(operands),
        out_specs=VMEM if single else [VMEM] * len(out_shape),
        scratch_shapes=list(scratch),
        cost_estimate=cost,
        compiler_params=pltpu.CompilerParams(vmem_limit_bytes=int(vmem * 2**20)),
    )(*operands)


def exchange_shards(bq, bk, bv, sq, sk, sv, br, sr, guidance):
    n, cores = lax.axis_size("seq"), lax.axis_size("head")
    tokens, small_tokens = bq.shape[0], sq.shape[0]
    group = bq.shape[1] // DH // n
    lat = br.shape[1]
    rows = row_layout(group, tokens, small_tokens)
    block = jax.ShapeDtypeStruct((rows["all"], DH), BF16)
    sources = [
        pltpu.with_memory_space_constraint(a, pltpu.HBM)
        for a in (bq, bk, bv, sq, sk, sv, br.T, sr.T)
    ]
    sent = call(
        functools.partial(pack_kernel, n, group),
        [block] * n,
        sources,
        specs=[pl.BlockSpec(memory_space=pltpu.HBM)] * len(sources),
        scratch=[pltpu.VMEM(a.shape, a.dtype) for a in sources]
        + [pltpu.SemaphoreType.DMA((len(sources),))],
    )
    hops = hop_order(n)
    blocks = [sent[0]]
    for k in hops[1:]:
        blocks.append(lax.ppermute(sent[k], "seq", [(j, j ^ k) for j in range(n)]))
    own_kv = call(
        functools.partial(gather_small_kernel, n, rows["sk"], 2 * small_tokens),
        jax.ShapeDtypeStruct((n * 2 * small_tokens, DH), BF16),
        blocks,
    )
    other_kv = lax.ppermute(own_kv, "head", [(c, c ^ 1) for c in range(cores)])
    big = call(
        functools.partial(big_kernel, n, group, tokens, lat, rows),
        jax.ShapeDtypeStruct((n * tokens, lat), F32),
        blocks,
        cost=pl.CostEstimate(flops=10**9, bytes_accessed=10**6, transcendentals=10**5),
    )
    partial = call(
        functools.partial(small_kernel, n, tokens, small_tokens, lat, rows, cores),
        jax.ShapeDtypeStruct((n * cores, tokens // 2, 2 * lat), BF16),
        (*blocks, own_kv, other_kv, big, guidance),
        specs=[VMEM] * (n + 3) + [SMEM],
        scratch=[pltpu.VMEM((n * tokens, DH), F32)],
    )
    terms = lax.all_to_all(partial, ("seq", "head"), split_axis=0, concat_axis=0, tiled=True)
    return call(
        sum_kernel, jax.ShapeDtypeStruct((tokens // 2, 2 * lat), F32), (terms,)
    )


def fits_exchange(mesh, bq, sq, br):
    groups, n, cores = mesh.shape["groups"], mesh.shape["seq"], mesh.shape["head"]
    tokens = bq.shape[0] // (groups * n)
    small_tokens = sq.shape[0] // (groups * n * cores)
    big_heads, small_heads = bq.shape[1] // DH // cores, sq.shape[1] // DH
    lat = br.shape[1]
    return (
        cores == 2
        and n & (n - 1) == 0
        and small_heads == n
        and big_heads % n == 0
        and big_heads // n * lat == DH
        and 2 * lat == DH
        and tokens % 32 == 0
        and small_tokens % 16 == 0
        and n * tokens <= 1024
    )


def split_heads(matrix, blocks, parts):
    rows_here, columns = matrix.shape
    shaped = matrix.reshape(blocks, rows_here // blocks, parts, columns // parts)
    shaped = jnp.transpose(shaped, (0, 2, 1, 3))
    return shaped.reshape(blocks * parts, rows_here // blocks, columns // parts)


def copy_heads(matrix, blocks, parts):
    rows_here, columns = matrix.shape
    shaped = jnp.transpose(matrix.reshape(rows_here, parts, columns // parts), (1, 0, 2))
    shaped = jnp.broadcast_to(shaped[None], (blocks, parts, rows_here, columns // parts))
    return shaped.reshape(blocks * parts, rows_here, columns // parts)


def join_heads(stacked, blocks, parts):
    pieces, rows_here, columns = stacked.shape
    shaped = stacked.reshape(blocks, parts, rows_here, columns)
    shaped = jnp.transpose(shaped, (0, 2, 1, 3))
    return shaped.reshape(blocks * rows_here, parts * columns)


def attend(query_rows, key_rows, value_rows):
    query_count = query_rows.shape[0]
    heads_here = query_rows.shape[1] // DH
    key_count = key_rows.shape[0]
    block_height = math.gcd(query_count, 256)
    block_count = query_count // block_height
    query_blocks = query_rows.reshape(block_count, block_height, heads_here, DH)
    key_split = key_rows.reshape(key_count, heads_here, DH)
    value_split = value_rows.reshape(key_count, heads_here, DH)
    score_scale = 1.0 / math.sqrt(DH)

    def one_block(query_block):
        scores = (
            jnp.einsum("qgd,kgd->gqk", query_block, key_split, preferred_element_type=F32)
            * score_scale
        )
        row_max = jnp.max(scores, axis=2, keepdims=True)
        probs = jnp.exp(scores - row_max)
        totals = jnp.sum(probs, axis=2, keepdims=True)
        weights = probs.astype(BF16)
        accumulated = jnp.einsum(
            "gqk,kgd->gqd", weights, value_split, preferred_element_type=F32
        )
        attended = accumulated / totals
        attended = jnp.transpose(attended, (1, 0, 2)).reshape(block_height, heads_here * DH)
        return attended.astype(BF16)

    outputs = lax.map(one_block, query_blocks)
    return outputs.reshape(query_count, heads_here * DH)


def seq_exchange(stacked, split, concat):
    return lax.all_to_all(stacked, "seq", split_axis=split, concat_axis=concat, tiled=True)


def run_model(queries, keys, values, shared):
    seq_count = lax.axis_size("seq")
    heads = queries.shape[1] // DH
    blocks = max(seq_count // heads, 1)
    parts = heads // max(heads // seq_count, 1)
    query_rows = seq_exchange(split_heads(queries, blocks, parts), 0, 1)[0]
    key_rows = seq_exchange(copy_heads(keys, blocks, parts), 0, 1)[0]
    value_rows = seq_exchange(copy_heads(values, blocks, parts), 0, 1)[0]
    if shared:
        key_rows = lax.all_gather(key_rows, "head", axis=0, tiled=True)
        value_rows = lax.all_gather(value_rows, "head", axis=0, tiled=True)
    out = attend(query_rows, key_rows, value_rows)
    return join_heads(seq_exchange(out[None], 1, 0), blocks, parts)


def general_shards(bq, bk, bv, sq, sk, sv, br, sr, guidance):
    big_attention = run_model(bq, bk, bv, False)
    big_partial = jnp.dot(big_attention, br, preferred_element_type=F32)
    small_attention = run_model(sq, sk, sv, True)
    small_latent = jnp.dot(small_attention, sr, preferred_element_type=F32)
    weight_value = guidance[0]
    core_index = lax.axis_index("head")
    placed = lax.dynamic_update_slice(
        jnp.zeros_like(big_partial),
        small_latent,
        (core_index * small_latent.shape[0], jnp.zeros((), jnp.int32)),
    )
    blended = lax.psum((1.0 + weight_value) * big_partial - weight_value * placed, "head")
    return blended.reshape(blended.shape[0] // 2, 2 * blended.shape[1])


def solution(mesh):
    placed = (
        P(("groups", "seq"), "head"),
        P(("groups", "seq"), "head"),
        P(("groups", "seq"), "head"),
        P(("groups", "seq", "head"), None),
        P(("groups", "seq", "head"), None),
        P(("groups", "seq", "head"), None),
        P("head", None),
        P(),
        P("groups"),
    )

    def whole(*arrays):
        fits = fits_exchange(mesh, arrays[0], arrays[3], arrays[6])
        return jax.shard_map(
            exchange_shards if fits else general_shards,
            mesh=mesh,
            in_specs=placed,
            out_specs=P(("groups", "seq"), None),
            check_vma=False,
        )(*arrays)

    return whole
```

```python
import functools
import math

import jax
import jax.numpy as jnp
from jax import lax
from jax.experimental import pallas as pl
from jax.experimental.pallas import tpu as pltpu
from jax.sharding import PartitionSpec as P

DH = 128
BF16 = jnp.bfloat16
F32 = jnp.float32
VMEM = pl.BlockSpec(memory_space=pltpu.VMEM)
HBM = pl.BlockSpec(memory_space=pltpu.HBM)
SMEM = pl.BlockSpec(memory_space=pltpu.SMEM)
NT = (((1,), (1,)), ((), ()))


def near_count(n):
    return n // 2


def hop_order(n):
    return [0] + [2, 4, 1, 7, 3, 5, 6] if n == 8 else list(range(n))


def row_layout(group, small_group, tokens, small_tokens):
    rows = {}
    at = 0
    for name, count in (
        ("k", group * tokens),
        ("vr", group // 2 * tokens),
        ("sk", small_group * small_tokens),
        ("svr", small_tokens),
        ("far", 0),
        ("q", group * tokens),
        ("sq", small_group * small_tokens),
        ("near", 0),
    ):
        rows[name] = at
        at += count
    return rows


def pack_kernel(n, near, group, small_group, rows, *refs):
    sources, outs, held, done = refs[:8], refs[8 : 8 + n], refs[8 + n : 16 + n], refs[16 + n]
    copies = [pltpu.make_async_copy(sources[i], held[i], done.at[i]) for i in range(8)]
    for copy in copies:
        copy.start()
    bk, bq, bv, br, sk, sq, sv, sr = held
    tokens, small_tokens = bk.shape[0], sk.shape[0]
    me = lax.axis_index("seq")

    def columns(j, heads, g):
        first = jnp.bitwise_xor(me, j) % near * heads + g
        return pl.ds(pl.multiple_of(first * DH, DH), DH)

    def put(j, row, value):
        for k in range(j, n, near):
            outs[k][pl.ds(row, value.shape[0]), :] = value

    copies[0].wait()
    for j in range(near):
        for g in range(group):
            put(j, rows["k"] + g * tokens, bk[:, columns(j, group, g)])
    copies[1].wait()
    for j in range(near):
        for g in range(group):
            outs[j][pl.ds(rows["q"] + g * tokens, tokens), :] = bq[:, columns(j, group, g)]
    copies[2].wait()
    copies[3].wait()
    for j in range(near):
        for g in range(0, group, 2):
            pair = []
            for h in (g, g + 1):
                cols = columns(j, group, h)
                pair.append(
                    lax.dot_general(bv[:, cols], br[:, cols], NT, preferred_element_type=F32)
                )
            put(j, rows["vr"] + g // 2 * tokens, jnp.concatenate(pair, axis=1).astype(BF16))
    for i in range(4, 8):
        copies[i].wait()
    for j in range(near):
        pair = []
        for g in range(small_group):
            cols = columns(j, small_group, g)
            put(j, rows["sk"] + g * small_tokens, sk[:, cols])
            outs[j][pl.ds(rows["sq"] + g * small_tokens, small_tokens), :] = sq[:, cols]
            pair.append(
                lax.dot_general(sv[:, cols], sr[:, cols], NT, preferred_element_type=F32)
            )
        put(j, rows["svr"], jnp.concatenate(pair, axis=1).astype(BF16))


def gather_small_kernel(order, near, rows, count, *refs):
    n = len(order)
    blocks, out = refs[:n], refs[n]
    other = 1 - lax.axis_index("head")
    at = 0

    def move(block, first):
        nonlocal at
        out[pl.ds(at, count), :] = block[pl.ds(first, count), :]
        at += count

    of_head = lambda name: pl.multiple_of(rows[name] + other * count, count)
    for block in blocks:
        move(block, of_head("sk"))
    for block in blocks:
        move(block, rows["svr"])
    for i in range(n):
        if order[i] < near:
            move(blocks[i], of_head("sq"))


def attend_head(queries, keys, values):
    scores = lax.dot_general(queries, keys, NT, preferred_element_type=F32)
    scores = scores * (1.0 / math.sqrt(DH))
    probs = jnp.exp(scores - jnp.max(scores, axis=1, keepdims=True))
    totals = jnp.sum(probs, axis=1, keepdims=True)
    out = jnp.dot(probs.astype(BF16), values, preferred_element_type=F32)
    return out / totals


def big_kernel(order, near, group, tokens, lat, rows, *refs):
    n = len(order)
    blocks, out = refs[:n], refs[n]
    here = [b for b, k in zip(blocks, order) if k < near]
    read = lambda some, first: jnp.concatenate(
        [b[pl.ds(first, tokens), :] for b in some], axis=0
    )
    total = None
    for g in range(group):
        if g % 2 == 0:
            values = read(blocks, rows["vr"] + g // 2 * tokens)
        part = attend_head(
            read(here, rows["q"] + g * tokens),
            read(blocks, rows["k"] + g * tokens),
            values[:, g % 2 * lat : (g % 2 + 1) * lat],
        )
        total = part if total is None else total + part
    out[:, :] = total


def small_kernel(order, near, tokens, count, lat, rows, *refs):
    n = len(order)
    blocks = refs[:n]
    theirs, big, guidance, out, latent = refs[n:]
    me, core = lax.axis_index("seq"), lax.axis_index("head")
    weight = guidance[0]
    here = [b for b, k in zip(blocks, order) if k < near]
    of_head = lambda name: pl.multiple_of(rows[name] + core * count, count)
    read = lambda some, first: [b[pl.ds(first, count), :] for b in some]
    join = lambda parts: jnp.concatenate(parts, axis=0)
    keys = join(read(blocks, of_head("sk")) + [theirs[: n * count, :]])
    values = join(read(blocks, rows["svr"]) + [theirs[n * count : 2 * n * count, :]])
    queries = join(read(here, of_head("sq")) + [theirs[2 * n * count :, :]])
    both = attend_head(queries, keys, values)
    small = weight * jnp.where(core == 0, both[:, :lat], both[:, lat : 2 * lat])
    latent[:, :lat] = (1.0 + weight) * big[:, :]
    for i in range(near):
        for side, whose in ((core, i), (1 - core, near + i)):
            part = pl.ds(pl.multiple_of(i * tokens + side * count, count), count)
            term = small[whose * count : (whose + 1) * count, :]
            latent[part, :lat] = latent[part, :lat] - term
    cores = tokens // count
    hops = [k for k in order if k < near]
    for i in range(near):
        even = latent[pl.ds(i * tokens, tokens // 2, stride=2), :lat]
        odd = latent[pl.ds(i * tokens + 1, tokens // 2, stride=2), :lat]
        dest = jnp.bitwise_xor(me, hops[i]) % near
        for c in range(cores):
            out[dest * cores + c] = jnp.concatenate([even, odd], axis=1)


def sum_kernel(x, out):
    total = x[0]
    for i in range(1, x.shape[0]):
        total = total + x[i]
    out[:, :] = total


def call(kernel, out_shape, operands, specs=None, scratch=(), cost=None):
    single = not isinstance(out_shape, (list, tuple))
    return pl.pallas_call(
        kernel,
        out_shape=out_shape,
        in_specs=specs if specs is not None else [VMEM] * len(operands),
        out_specs=VMEM if single else [VMEM] * len(out_shape),
        scratch_shapes=list(scratch),
        cost_estimate=cost,
        compiler_params=pltpu.CompilerParams(vmem_limit_bytes=16 * 2**20),
    )(*operands)


def exchange_shards(bq, bk, bv, sq, sk, sv, br, sr, guidance):
    n, cores = lax.axis_size("seq"), lax.axis_size("head")
    near = near_count(n)
    order = hop_order(n)
    tokens, count = bq.shape[0], sq.shape[0]
    group, small_group = bq.shape[1] // DH // near, sq.shape[1] // DH // near
    lat = br.shape[1]
    rows = row_layout(group, small_group, tokens, count)
    shape = lambda *dims, dtype=BF16: jax.ShapeDtypeStruct(dims, dtype)
    sources = [
        pltpu.with_memory_space_constraint(a, pltpu.HBM)
        for a in (bk, bq, bv, br.T, sk, sq, sv, sr.T)
    ]
    sent = call(
        functools.partial(pack_kernel, n, near, group, small_group, rows),
        [shape(rows["near" if k < near else "far"], DH) for k in range(n)],
        sources,
        specs=[HBM] * len(sources),
        scratch=[pltpu.VMEM(a.shape, a.dtype) for a in sources]
        + [pltpu.SemaphoreType.DMA((len(sources),))],
    )
    blocks = [sent[0]]
    for k in order[1:]:
        blocks.append(lax.ppermute(sent[k], "seq", [(j, j ^ k) for j in range(n)]))
    ours = call(
        functools.partial(gather_small_kernel, order, near, rows, count),
        shape((2 * n + near) * count, DH),
        blocks,
    )
    theirs = lax.ppermute(ours, "head", [(c, c ^ 1) for c in range(cores)])
    big = call(
        functools.partial(big_kernel, order, near, group, tokens, lat, rows),
        shape(near * tokens, lat, dtype=F32),
        blocks,
        cost=pl.CostEstimate(flops=10**9, bytes_accessed=10**6, transcendentals=10**5),
    )
    partial = call(
        functools.partial(small_kernel, order, near, tokens, count, lat, rows),
        shape(near * cores, tokens // 2, 2 * lat, dtype=F32),
        (*blocks, theirs, big, guidance),
        specs=[VMEM] * (n + 2) + [SMEM],
        scratch=[pltpu.VMEM((near * tokens, DH), F32)],
    )
    size = near * cores
    terms = lax.all_to_all(
        partial,
        ("seq", "head"),
        split_axis=0,
        concat_axis=0,
        tiled=True,
        axis_index_groups=[
            list(range(first, first + size)) for first in range(0, n * cores, size)
        ],
    )
    return call(sum_kernel, shape(tokens // 2, 2 * lat, dtype=F32), (terms,))


def fits_exchange(mesh, bq, sq, br):
    groups, n, cores = mesh.shape["groups"], mesh.shape["seq"], mesh.shape["head"]
    near = near_count(n)
    tokens = bq.shape[0] // (groups * n)
    count = sq.shape[0] // (groups * n * cores)
    big_heads, small_heads = bq.shape[1] // DH // cores, sq.shape[1] // DH
    return (
        cores == 2
        and n & (n - 1) == 0
        and near >= 1
        and small_heads == near * cores
        and big_heads % (2 * near) == 0
        and 2 * br.shape[1] == DH
        and count % 16 == 0
        and n * tokens <= 1024
    )


def split_heads(matrix, blocks, parts):
    rows_here, columns = matrix.shape
    shaped = matrix.reshape(blocks, rows_here // blocks, parts, columns // parts)
    shaped = jnp.transpose(shaped, (0, 2, 1, 3))
    return shaped.reshape(blocks * parts, rows_here // blocks, columns // parts)


def copy_heads(matrix, blocks, parts):
    rows_here, columns = matrix.shape
    shaped = jnp.transpose(matrix.reshape(rows_here, parts, columns // parts), (1, 0, 2))
    shaped = jnp.broadcast_to(shaped[None], (blocks, parts, rows_here, columns // parts))
    return shaped.reshape(blocks * parts, rows_here, columns // parts)


def join_heads(stacked, blocks, parts):
    pieces, rows_here, columns = stacked.shape
    shaped = stacked.reshape(blocks, parts, rows_here, columns)
    shaped = jnp.transpose(shaped, (0, 2, 1, 3))
    return shaped.reshape(blocks * rows_here, parts * columns)


def attend(query_rows, key_rows, value_rows):
    query_count = query_rows.shape[0]
    heads_here = query_rows.shape[1] // DH
    key_count = key_rows.shape[0]
    block_height = math.gcd(query_count, 256)
    block_count = query_count // block_height
    query_blocks = query_rows.reshape(block_count, block_height, heads_here, DH)
    key_split = key_rows.reshape(key_count, heads_here, DH)
    value_split = value_rows.reshape(key_count, heads_here, DH)
    score_scale = 1.0 / math.sqrt(DH)

    def one_block(query_block):
        scores = (
            jnp.einsum("qgd,kgd->gqk", query_block, key_split, preferred_element_type=F32)
            * score_scale
        )
        row_max = jnp.max(scores, axis=2, keepdims=True)
        probs = jnp.exp(scores - row_max)
        totals = jnp.sum(probs, axis=2, keepdims=True)
        weights = probs.astype(BF16)
        accumulated = jnp.einsum(
            "gqk,kgd->gqd", weights, value_split, preferred_element_type=F32
        )
        attended = accumulated / totals
        attended = jnp.transpose(attended, (1, 0, 2)).reshape(block_height, heads_here * DH)
        return attended.astype(BF16)

    outputs = lax.map(one_block, query_blocks)
    return outputs.reshape(query_count, heads_here * DH)


def seq_exchange(stacked, split, concat):
    return lax.all_to_all(stacked, "seq", split_axis=split, concat_axis=concat, tiled=True)


def run_model(queries, keys, values, shared):
    seq_count = lax.axis_size("seq")
    heads = queries.shape[1] // DH
    blocks = max(seq_count // heads, 1)
    parts = heads // max(heads // seq_count, 1)
    query_rows = seq_exchange(split_heads(queries, blocks, parts), 0, 1)[0]
    key_rows = seq_exchange(copy_heads(keys, blocks, parts), 0, 1)[0]
    value_rows = seq_exchange(copy_heads(values, blocks, parts), 0, 1)[0]
    if shared:
        key_rows = lax.all_gather(key_rows, "head", axis=0, tiled=True)
        value_rows = lax.all_gather(value_rows, "head", axis=0, tiled=True)
    out = attend(query_rows, key_rows, value_rows)
    return join_heads(seq_exchange(out[None], 1, 0), blocks, parts)


def general_shards(bq, bk, bv, sq, sk, sv, br, sr, guidance):
    big_attention = run_model(bq, bk, bv, False)
    big_partial = jnp.dot(big_attention, br, preferred_element_type=F32)
    small_attention = run_model(sq, sk, sv, True)
    small_latent = jnp.dot(small_attention, sr, preferred_element_type=F32)
    weight_value = guidance[0]
    core_index = lax.axis_index("head")
    placed = lax.dynamic_update_slice(
        jnp.zeros_like(big_partial),
        small_latent,
        (core_index * small_latent.shape[0], jnp.zeros((), jnp.int32)),
    )
    blended = lax.psum((1.0 + weight_value) * big_partial - weight_value * placed, "head")
    return blended.reshape(blended.shape[0] // 2, 2 * blended.shape[1])


def solution(mesh):
    placed = (
        P(("groups", "seq"), "head"),
        P(("groups", "seq"), "head"),
        P(("groups", "seq"), "head"),
        P(("groups", "seq", "head"), None),
        P(("groups", "seq", "head"), None),
        P(("groups", "seq", "head"), None),
        P("head", None),
        P(),
        P("groups"),
    )

    def whole(*arrays):
        fits = fits_exchange(mesh, arrays[0], arrays[3], arrays[6])
        return jax.shard_map(
            exchange_shards if fits else general_shards,
            mesh=mesh,
            in_specs=placed,
            out_specs=P(("groups", "seq"), None),
            check_vma=False,
        )(*arrays)

    return whole
```

```python
import functools
import math

import jax
import jax.numpy as jnp
from jax import lax
from jax.experimental import pallas as pl
from jax.experimental.pallas import tpu as pltpu
from jax.sharding import PartitionSpec as P

DH = 128
BF16 = jnp.bfloat16
F32 = jnp.float32
VMEM = pl.BlockSpec(memory_space=pltpu.VMEM)
HBM = pl.BlockSpec(memory_space=pltpu.HBM)
SMEM = pl.BlockSpec(memory_space=pltpu.SMEM)
NT = (((1,), (1,)), ((), ()))


def near_count(n):
    return n // 2


def hop_order(n):
    return [0] + [2, 4, 1, 7, 3, 5, 6] if n == 8 else list(range(n))


def row_layout(group, small_group, tokens, small_tokens):
    rows = {}
    at = 0
    for name, count in (
        ("k", group * tokens),
        ("vr", group // 2 * tokens),
        ("sk", small_group * small_tokens),
        ("svr", small_tokens),
        ("far", 0),
        ("q", group * tokens),
        ("sq", small_group * small_tokens),
        ("near", 0),
    ):
        rows[name] = at
        at += count
    return rows


def pack_kernel(n, near, group, small_group, rows, *refs):
    sources, outs, held, done = refs[:8], refs[8 : 8 + n], refs[8 + n : 16 + n], refs[16 + n]
    copies = [pltpu.make_async_copy(sources[i], held[i], done.at[i]) for i in range(8)]
    for copy in copies:
        copy.start()
    sv, sr, bv, br, sk, sq, bk, bq = held
    tokens, small_tokens = bk.shape[0], sk.shape[0]
    me = lax.axis_index("seq")

    def columns(j, heads, g):
        first = jnp.bitwise_xor(me, j) % near * heads + g
        return pl.ds(pl.multiple_of(first * DH, DH), DH)

    def put(j, row, value):
        for k in range(j, n, near):
            outs[k][pl.ds(row, value.shape[0]), :] = value

    def project(values, readout, heads, j, g):
        first = jnp.bitwise_xor(me, j) % near * heads + g
        cols = pl.ds(pl.multiple_of(first * DH, DH), 2 * DH)
        pair = readout[:, cols]
        none = jnp.zeros((readout.shape[0], DH), BF16)
        left = jnp.concatenate([pair[:, :DH], none], axis=1)
        right = jnp.concatenate([none, pair[:, DH:]], axis=1)
        both = jnp.concatenate([left, right], axis=0)
        out = lax.dot_general(values[:, cols], both, NT, preferred_element_type=F32)
        return out.astype(BF16)

    copies[0].wait()
    copies[1].wait()
    for j in range(near):
        put(j, rows["svr"], project(sv, sr, small_group, j, 0))
    copies[2].wait()
    copies[3].wait()
    for j in range(near):
        for g in range(0, group, 2):
            put(j, rows["vr"] + g // 2 * tokens, project(bv, br, group, j, g))
    copies[4].wait()
    copies[5].wait()
    for j in range(near):
        for g in range(small_group):
            cols = columns(j, small_group, g)
            put(j, rows["sk"] + g * small_tokens, sk[:, cols])
            outs[j][pl.ds(rows["sq"] + g * small_tokens, small_tokens), :] = sq[:, cols]
    copies[6].wait()
    copies[7].wait()
    for j in range(near):
        for g in range(group):
            cols = columns(j, group, g)
            put(j, rows["k"] + g * tokens, bk[:, cols])
            outs[j][pl.ds(rows["q"] + g * tokens, tokens), :] = bq[:, cols]


def gather_small_kernel(order, near, rows, count, *refs):
    n = len(order)
    blocks, out = refs[:n], refs[n]
    other = 1 - lax.axis_index("head")
    at = 0

    def move(block, first):
        nonlocal at
        out[pl.ds(at, count), :] = block[pl.ds(first, count), :]
        at += count

    of_head = lambda name: pl.multiple_of(rows[name] + other * count, count)
    for block in blocks:
        move(block, of_head("sk"))
    for block in blocks:
        move(block, rows["svr"])
    for i in range(n):
        if order[i] < near:
            move(blocks[i], of_head("sq"))


def attend_head(queries, keys, values):
    scores = lax.dot_general(queries, keys, NT, preferred_element_type=F32)
    scores = scores * (1.0 / math.sqrt(DH))
    probs = jnp.exp(scores - jnp.max(scores, axis=1, keepdims=True))
    totals = jnp.sum(probs, axis=1, keepdims=True)
    out = jnp.dot(probs.astype(BF16), values, preferred_element_type=F32)
    return out / totals


def big_kernel(order, near, group, tokens, lat, rows, *refs):
    n = len(order)
    blocks, out = refs[:n], refs[n]
    here = [b for b, k in zip(blocks, order) if k < near]
    read = lambda some, first: jnp.concatenate(
        [b[pl.ds(first, tokens), :] for b in some], axis=0
    )
    total = None
    for g in range(group):
        if g % 2 == 0:
            values = read(blocks, rows["vr"] + g // 2 * tokens)
        part = attend_head(
            read(here, rows["q"] + g * tokens),
            read(blocks, rows["k"] + g * tokens),
            values[:, g % 2 * lat : (g % 2 + 1) * lat],
        )
        total = part if total is None else total + part
    out[:, :] = total


def small_kernel(order, near, tokens, count, lat, rows, *refs):
    n = len(order)
    blocks = refs[:n]
    theirs, big, guidance, out, latent = refs[n:]
    me, core = lax.axis_index("seq"), lax.axis_index("head")
    weight = guidance[0]
    here = [b for b, k in zip(blocks, order) if k < near]
    of_head = lambda name: pl.multiple_of(rows[name] + core * count, count)
    read = lambda some, first: [b[pl.ds(first, count), :] for b in some]
    join = lambda parts: jnp.concatenate(parts, axis=0)
    keys = join(read(blocks, of_head("sk")) + [theirs[: n * count, :]])
    values = join(read(blocks, rows["svr"]) + [theirs[n * count : 2 * n * count, :]])
    queries = join(read(here, of_head("sq")) + [theirs[2 * n * count :, :]])
    both = attend_head(queries, keys, values)
    small = weight * jnp.where(core == 0, both[:, :lat], both[:, lat : 2 * lat])
    latent[:, :lat] = (1.0 + weight) * big[:, :]
    for i in range(near):
        for side, whose in ((core, i), (1 - core, near + i)):
            part = pl.ds(pl.multiple_of(i * tokens + side * count, count), count)
            term = small[whose * count : (whose + 1) * count, :]
            latent[part, :lat] = latent[part, :lat] - term
    cores = tokens // count
    hops = [k for k in order if k < near]
    for i in range(near):
        even = latent[pl.ds(i * tokens, tokens // 2, stride=2), :lat]
        odd = latent[pl.ds(i * tokens + 1, tokens // 2, stride=2), :lat]
        dest = jnp.bitwise_xor(me, hops[i]) % near
        for c in range(cores):
            out[dest * cores + c] = jnp.concatenate([even, odd], axis=1)


def sum_kernel(x, out):
    total = x[0]
    for i in range(1, x.shape[0]):
        total = total + x[i]
    out[:, :] = total


def call(kernel, out_shape, operands, specs=None, scratch=(), cost=None):
    single = not isinstance(out_shape, (list, tuple))
    return pl.pallas_call(
        kernel,
        out_shape=out_shape,
        in_specs=specs if specs is not None else [VMEM] * len(operands),
        out_specs=VMEM if single else [VMEM] * len(out_shape),
        scratch_shapes=list(scratch),
        cost_estimate=cost,
        compiler_params=pltpu.CompilerParams(vmem_limit_bytes=16 * 2**20),
    )(*operands)


def exchange_shards(bq, bk, bv, sq, sk, sv, br, sr, guidance):
    n, cores = lax.axis_size("seq"), lax.axis_size("head")
    near = near_count(n)
    order = hop_order(n)
    tokens, count = bq.shape[0], sq.shape[0]
    group, small_group = bq.shape[1] // DH // near, sq.shape[1] // DH // near
    lat = br.shape[1]
    rows = row_layout(group, small_group, tokens, count)
    shape = lambda *dims, dtype=BF16: jax.ShapeDtypeStruct(dims, dtype)
    sources = [
        pltpu.with_memory_space_constraint(a, pltpu.HBM)
        for a in (sv, sr.T, bv, br.T, sk, sq, bk, bq)
    ]
    sent = call(
        functools.partial(pack_kernel, n, near, group, small_group, rows),
        [shape(rows["near" if k < near else "far"], DH) for k in range(n)],
        sources,
        specs=[HBM] * len(sources),
        scratch=[pltpu.VMEM(a.shape, a.dtype) for a in sources]
        + [pltpu.SemaphoreType.DMA((len(sources),))],
    )
    blocks = [sent[0]]
    for k in order[1:]:
        blocks.append(lax.ppermute(sent[k], "seq", [(j, j ^ k) for j in range(n)]))
    ours = call(
        functools.partial(gather_small_kernel, order, near, rows, count),
        shape((2 * n + near) * count, DH),
        blocks,
    )
    theirs = lax.ppermute(ours, "head", [(c, c ^ 1) for c in range(cores)])
    big = call(
        functools.partial(big_kernel, order, near, group, tokens, lat, rows),
        shape(near * tokens, lat, dtype=F32),
        blocks,
        cost=pl.CostEstimate(flops=10**9, bytes_accessed=10**6, transcendentals=10**5),
    )
    partial = call(
        functools.partial(small_kernel, order, near, tokens, count, lat, rows),
        shape(near * cores, tokens // 2, 2 * lat, dtype=F32),
        (*blocks, theirs, big, guidance),
        specs=[VMEM] * (n + 2) + [SMEM],
        scratch=[pltpu.VMEM((near * tokens, DH), F32)],
    )
    size = near * cores
    terms = lax.all_to_all(
        partial,
        ("seq", "head"),
        split_axis=0,
        concat_axis=0,
        tiled=True,
        axis_index_groups=[
            list(range(first, first + size)) for first in range(0, n * cores, size)
        ],
    )
    return call(sum_kernel, shape(tokens // 2, 2 * lat, dtype=F32), (terms,))


def fits_exchange(mesh, bq, sq, br):
    groups, n, cores = mesh.shape["groups"], mesh.shape["seq"], mesh.shape["head"]
    near = near_count(n)
    tokens = bq.shape[0] // (groups * n)
    count = sq.shape[0] // (groups * n * cores)
    big_heads, small_heads = bq.shape[1] // DH // cores, sq.shape[1] // DH
    return (
        cores == 2
        and n & (n - 1) == 0
        and near >= 1
        and small_heads == near * cores
        and big_heads % (2 * near) == 0
        and 2 * br.shape[1] == DH
        and count % 16 == 0
        and n * tokens <= 1024
    )


def split_heads(matrix, blocks, parts):
    rows_here, columns = matrix.shape
    shaped = matrix.reshape(blocks, rows_here // blocks, parts, columns // parts)
    shaped = jnp.transpose(shaped, (0, 2, 1, 3))
    return shaped.reshape(blocks * parts, rows_here // blocks, columns // parts)


def copy_heads(matrix, blocks, parts):
    rows_here, columns = matrix.shape
    shaped = jnp.transpose(matrix.reshape(rows_here, parts, columns // parts), (1, 0, 2))
    shaped = jnp.broadcast_to(shaped[None], (blocks, parts, rows_here, columns // parts))
    return shaped.reshape(blocks * parts, rows_here, columns // parts)


def join_heads(stacked, blocks, parts):
    pieces, rows_here, columns = stacked.shape
    shaped = stacked.reshape(blocks, parts, rows_here, columns)
    shaped = jnp.transpose(shaped, (0, 2, 1, 3))
    return shaped.reshape(blocks * rows_here, parts * columns)


def attend(query_rows, key_rows, value_rows):
    query_count = query_rows.shape[0]
    heads_here = query_rows.shape[1] // DH
    key_count = key_rows.shape[0]
    block_height = math.gcd(query_count, 256)
    block_count = query_count // block_height
    query_blocks = query_rows.reshape(block_count, block_height, heads_here, DH)
    key_split = key_rows.reshape(key_count, heads_here, DH)
    value_split = value_rows.reshape(key_count, heads_here, DH)
    score_scale = 1.0 / math.sqrt(DH)

    def one_block(query_block):
        scores = (
            jnp.einsum("qgd,kgd->gqk", query_block, key_split, preferred_element_type=F32)
            * score_scale
        )
        row_max = jnp.max(scores, axis=2, keepdims=True)
        probs = jnp.exp(scores - row_max)
        totals = jnp.sum(probs, axis=2, keepdims=True)
        weights = probs.astype(BF16)
        accumulated = jnp.einsum(
            "gqk,kgd->gqd", weights, value_split, preferred_element_type=F32
        )
        attended = accumulated / totals
        attended = jnp.transpose(attended, (1, 0, 2)).reshape(block_height, heads_here * DH)
        return attended.astype(BF16)

    outputs = lax.map(one_block, query_blocks)
    return outputs.reshape(query_count, heads_here * DH)


def seq_exchange(stacked, split, concat):
    return lax.all_to_all(stacked, "seq", split_axis=split, concat_axis=concat, tiled=True)


def run_model(queries, keys, values, shared):
    seq_count = lax.axis_size("seq")
    heads = queries.shape[1] // DH
    blocks = max(seq_count // heads, 1)
    parts = heads // max(heads // seq_count, 1)
    query_rows = seq_exchange(split_heads(queries, blocks, parts), 0, 1)[0]
    key_rows = seq_exchange(copy_heads(keys, blocks, parts), 0, 1)[0]
    value_rows = seq_exchange(copy_heads(values, blocks, parts), 0, 1)[0]
    if shared:
        key_rows = lax.all_gather(key_rows, "head", axis=0, tiled=True)
        value_rows = lax.all_gather(value_rows, "head", axis=0, tiled=True)
    out = attend(query_rows, key_rows, value_rows)
    return join_heads(seq_exchange(out[None], 1, 0), blocks, parts)


def general_shards(bq, bk, bv, sq, sk, sv, br, sr, guidance):
    big_attention = run_model(bq, bk, bv, False)
    big_partial = jnp.dot(big_attention, br, preferred_element_type=F32)
    small_attention = run_model(sq, sk, sv, True)
    small_latent = jnp.dot(small_attention, sr, preferred_element_type=F32)
    weight_value = guidance[0]
    core_index = lax.axis_index("head")
    placed = lax.dynamic_update_slice(
        jnp.zeros_like(big_partial),
        small_latent,
        (core_index * small_latent.shape[0], jnp.zeros((), jnp.int32)),
    )
    blended = lax.psum((1.0 + weight_value) * big_partial - weight_value * placed, "head")
    return blended.reshape(blended.shape[0] // 2, 2 * blended.shape[1])


def solution(mesh):
    placed = (
        P(("groups", "seq"), "head"),
        P(("groups", "seq"), "head"),
        P(("groups", "seq"), "head"),
        P(("groups", "seq", "head"), None),
        P(("groups", "seq", "head"), None),
        P(("groups", "seq", "head"), None),
        P("head", None),
        P(),
        P("groups"),
    )

    def whole(*arrays):
        fits = fits_exchange(mesh, arrays[0], arrays[3], arrays[6])
        return jax.shard_map(
            exchange_shards if fits else general_shards,
            mesh=mesh,
            in_specs=placed,
            out_specs=P(("groups", "seq"), None),
            check_vma=False,
        )(*arrays)

    return whole
```

```python
import functools
import math

import jax
import jax.numpy as jnp
from jax import lax
from jax.experimental import pallas as pl
from jax.experimental.pallas import tpu as pltpu
from jax.sharding import PartitionSpec as P

DH = 128
BF16 = jnp.bfloat16
F32 = jnp.float32
VMEM = pl.BlockSpec(memory_space=pltpu.VMEM)
HBM = pl.BlockSpec(memory_space=pltpu.HBM)
SMEM = pl.BlockSpec(memory_space=pltpu.SMEM)
NT = (((1,), (1,)), ((), ()))


def near_count(n):
    return n // 2


def hop_order(n):
    return [0] + [2, 4, 1, 7, 3, 5, 6] if n == 8 else list(range(n))


def row_layout(group, small_group, tokens, small_tokens):
    rows = {}
    at = 0
    for name, count in (
        ("k", group * tokens),
        ("vr", group // 2 * tokens),
        ("sk", small_group * small_tokens),
        ("svr", small_tokens),
        ("far", 0),
        ("q", group * tokens),
        ("sq", small_group * small_tokens),
        ("near", 0),
    ):
        rows[name] = at
        at += count
    return rows


def pack_kernel(n, near, group, small_group, rows, *refs):
    sources, outs, held, done = refs[:8], refs[8 : 8 + n], refs[8 + n : 16 + n], refs[16 + n]
    copies = [pltpu.make_async_copy(sources[i], held[i], done.at[i]) for i in range(8)]
    for copy in copies:
        copy.start()
    sv, sr, bv, br, sk, sq, bk, bq = held
    tokens, small_tokens = bk.shape[0], sk.shape[0]
    me = lax.axis_index("seq")

    def columns(j, heads, g):
        first = jnp.bitwise_xor(me, j) % near * heads + g
        return pl.ds(pl.multiple_of(first * DH, DH), DH)

    def put(j, row, value):
        for k in range(j, n, near):
            outs[k][pl.ds(row, value.shape[0]), :] = value

    def project(values, readout, heads, j, g):
        first = jnp.bitwise_xor(me, j) % near * heads + g
        cols = pl.ds(pl.multiple_of(first * DH, DH), 2 * DH)
        pair = readout[:, cols]
        none = jnp.zeros((readout.shape[0], DH), BF16)
        left = jnp.concatenate([pair[:, :DH], none], axis=1)
        right = jnp.concatenate([none, pair[:, DH:]], axis=1)
        both = jnp.concatenate([left, right], axis=0)
        out = lax.dot_general(values[:, cols], both, NT, preferred_element_type=F32)
        return out.astype(BF16)

    copies[0].wait()
    copies[1].wait()
    for j in range(near):
        put(j, rows["svr"], project(sv, sr, small_group, j, 0))
    copies[2].wait()
    copies[3].wait()
    for j in range(near):
        for g in range(0, group, 2):
            put(j, rows["vr"] + g // 2 * tokens, project(bv, br, group, j, g))
    copies[4].wait()
    copies[5].wait()
    for j in range(near):
        for g in range(small_group):
            cols = columns(j, small_group, g)
            put(j, rows["sk"] + g * small_tokens, sk[:, cols])
            outs[j][pl.ds(rows["sq"] + g * small_tokens, small_tokens), :] = sq[:, cols]
    copies[6].wait()
    copies[7].wait()
    for j in range(near):
        for g in range(group):
            cols = columns(j, group, g)
            put(j, rows["k"] + g * tokens, bk[:, cols])
            outs[j][pl.ds(rows["q"] + g * tokens, tokens), :] = bq[:, cols]


def gather_small_kernel(order, near, rows, *refs):
    n = len(order)
    blocks, (guidance, out, weight) = refs[:n], refs[n:]
    weight[:, :] = jnp.full(weight.shape, guidance[0], F32)
    at = 0
    for block, k in zip(blocks, order):
        parts = [(rows["sk"], rows["far"])] + ([(rows["sq"], rows["near"])] if k < near else [])
        for first, last in parts:
            out[pl.ds(at, last - first), :] = block[pl.ds(first, last - first), :]
            at += last - first


def attend_head(queries, keys, values):
    scores = lax.dot_general(queries, keys, NT, preferred_element_type=F32)
    scores = scores * (1.0 / math.sqrt(DH))
    probs = jnp.exp(scores - jnp.max(scores, axis=1, keepdims=True))
    totals = jnp.sum(probs, axis=1, keepdims=True)
    out = jnp.dot(probs.astype(BF16), values, preferred_element_type=F32)
    return out / totals


def big_kernel(order, near, group, tokens, lat, rows, *refs):
    n = len(order)
    blocks, out = refs[:n], refs[n]
    here = [b for b, k in zip(blocks, order) if k < near]
    read = lambda some, first: jnp.concatenate(
        [b[pl.ds(first, tokens), :] for b in some], axis=0
    )
    total = None
    for g in range(group):
        if g % 2 == 0:
            values = read(blocks, rows["vr"] + g // 2 * tokens)
        part = attend_head(
            read(here, rows["q"] + g * tokens),
            read(blocks, rows["k"] + g * tokens),
            values[:, g % 2 * lat : (g % 2 + 1) * lat],
        )
        total = part if total is None else total + part
    out[:, :] = total


def small_kernel(order, near, small_group, tokens, count, lat, rows, *refs):
    n = len(order)
    blocks, theirs, out = refs[:n], refs[n], refs[n + 1]
    core = lax.axis_index("head")
    at = 0
    found = {name: [] for name in ("sk", "svr", "sq")}
    for block, k in zip(blocks, order):
        for name, size in (
            ("sk", small_group * count),
            ("svr", count),
            ("sq", small_group * count),
        ):
            if name == "sq" and k >= near:
                continue
            own = block[pl.ds(rows[name], size), :]
            found[name].append((own, theirs[pl.ds(at, size), :]))
            at += size

    def read(name, first):
        sides = [[p[side][first : first + count] for p in found[name]] for side in (0, 1)]
        return jnp.concatenate(sides[0] + sides[1], axis=0)

    values = read("svr", 0)
    total = None
    for g in range(small_group):
        part = attend_head(
            read("sq", g * count), read("sk", g * count), values[:, g * lat : (g + 1) * lat]
        )
        total = part if total is None else total + part
    for i in range(near):
        for side, whose in ((core, i), (1 - core, near + i)):
            part = pl.ds(pl.multiple_of(i * tokens + side * count, count), count)
            out[part, :] = total[whose * count : (whose + 1) * count, :]


def blend_kernel(near, tokens, big, other_big, small, guidance, *refs):
    outs, latent = refs[:near], refs[near]
    lat = big.shape[1]
    weight = guidance[:1, :lat]
    latent[:, :lat] = (1.0 + weight) * (big[:, :] + other_big[:, :]) - weight * small[:, :]
    for i in range(near):
        even = latent[pl.ds(i * tokens, tokens // 2, stride=2), :lat]
        odd = latent[pl.ds(i * tokens + 1, tokens // 2, stride=2), :lat]
        outs[i][:, :] = jnp.concatenate([even, odd], axis=1)


def sum_kernel(*refs):
    total = refs[0][:, :]
    for x in refs[1:-1]:
        total = total + x[:, :]
    refs[-1][:, :] = total


def call(kernel, out_shape, operands, specs=None, scratch=(), cost=None):
    single = not isinstance(out_shape, (list, tuple))
    return pl.pallas_call(
        kernel,
        out_shape=out_shape,
        in_specs=specs if specs is not None else [VMEM] * len(operands),
        out_specs=VMEM if single else [VMEM] * len(out_shape),
        scratch_shapes=list(scratch),
        cost_estimate=cost,
        compiler_params=pltpu.CompilerParams(vmem_limit_bytes=16 * 2**20),
    )(*operands)


def exchange_shards(bq, bk, bv, sq, sk, sv, br, sr, guidance):
    n, cores = lax.axis_size("seq"), lax.axis_size("head")
    near = near_count(n)
    order = hop_order(n)
    tokens, count = bq.shape[0], sq.shape[0]
    group, small_group = bq.shape[1] // DH // near, sq.shape[1] // DH // near
    lat = br.shape[1]
    rows = row_layout(group, small_group, tokens, count)
    shape = lambda *dims, dtype=BF16: jax.ShapeDtypeStruct(dims, dtype)
    sources = [
        pltpu.with_memory_space_constraint(a, pltpu.HBM)
        for a in (sv, sr.T, bv, br.T, sk, sq, bk, bq)
    ]
    sent = call(
        functools.partial(pack_kernel, n, near, group, small_group, rows),
        [shape(rows["near" if k < near else "far"], DH) for k in range(n)],
        sources,
        specs=[HBM] * len(sources),
        scratch=[pltpu.VMEM(a.shape, a.dtype) for a in sources]
        + [pltpu.SemaphoreType.DMA((len(sources),))],
    )
    blocks = [sent[0]]
    for k in order[1:]:
        blocks.append(lax.ppermute(sent[k], "seq", [(j, j ^ k) for j in range(n)]))
    ours, weight = call(
        functools.partial(gather_small_kernel, order, near, rows),
        [
            shape(n * (rows["far"] - rows["sk"]) + near * (rows["near"] - rows["sq"]), DH),
            shape(8, DH, dtype=F32),
        ],
        (*blocks, guidance),
        specs=[VMEM] * n + [SMEM],
    )
    swap = lambda a: lax.ppermute(a, "head", [(c, c ^ 1) for c in range(cores)])
    theirs = swap(ours)
    big = call(
        functools.partial(big_kernel, order, near, group, tokens, lat, rows),
        shape(near * tokens, lat, dtype=F32),
        blocks,
        cost=pl.CostEstimate(flops=10**9, bytes_accessed=10**6, transcendentals=10**5),
    )
    other_big = swap(big)
    small = call(
        functools.partial(small_kernel, order, near, small_group, tokens, count, lat, rows),
        shape(near * tokens, lat, dtype=F32),
        (*blocks, theirs),
        cost=pl.CostEstimate(flops=10**9, bytes_accessed=10**6, transcendentals=10**5),
    )
    hops = [k for k in order if k < near]
    terms = call(
        functools.partial(blend_kernel, near, tokens),
        [shape(tokens // 2, 2 * lat, dtype=F32)] * near,
        (big, other_big, small, weight),
        scratch=[pltpu.VMEM((near * tokens, DH), F32)],
    )
    sums = [terms[0]]
    for i in range(1, near):
        sums.append(lax.ppermute(terms[i], "seq", [(j, j ^ hops[i]) for j in range(n)]))
    return call(sum_kernel, shape(tokens // 2, 2 * lat, dtype=F32), sums)


def fits_exchange(mesh, bq, sq, br):
    groups, n, cores = mesh.shape["groups"], mesh.shape["seq"], mesh.shape["head"]
    near = near_count(n)
    tokens = bq.shape[0] // (groups * n)
    count = sq.shape[0] // (groups * n * cores)
    big_heads, small_heads = bq.shape[1] // DH // cores, sq.shape[1] // DH
    return (
        cores == 2
        and n & (n - 1) == 0
        and near >= 1
        and small_heads == near * cores
        and big_heads % (2 * near) == 0
        and 2 * br.shape[1] == DH
        and count % 16 == 0
        and n * tokens <= 1024
    )


def split_heads(matrix, blocks, parts):
    rows_here, columns = matrix.shape
    shaped = matrix.reshape(blocks, rows_here // blocks, parts, columns // parts)
    shaped = jnp.transpose(shaped, (0, 2, 1, 3))
    return shaped.reshape(blocks * parts, rows_here // blocks, columns // parts)


def copy_heads(matrix, blocks, parts):
    rows_here, columns = matrix.shape
    shaped = jnp.transpose(matrix.reshape(rows_here, parts, columns // parts), (1, 0, 2))
    shaped = jnp.broadcast_to(shaped[None], (blocks, parts, rows_here, columns // parts))
    return shaped.reshape(blocks * parts, rows_here, columns // parts)


def join_heads(stacked, blocks, parts):
    pieces, rows_here, columns = stacked.shape
    shaped = stacked.reshape(blocks, parts, rows_here, columns)
    shaped = jnp.transpose(shaped, (0, 2, 1, 3))
    return shaped.reshape(blocks * rows_here, parts * columns)


def attend(query_rows, key_rows, value_rows):
    query_count = query_rows.shape[0]
    heads_here = query_rows.shape[1] // DH
    key_count = key_rows.shape[0]
    block_height = math.gcd(query_count, 256)
    block_count = query_count // block_height
    query_blocks = query_rows.reshape(block_count, block_height, heads_here, DH)
    key_split = key_rows.reshape(key_count, heads_here, DH)
    value_split = value_rows.reshape(key_count, heads_here, DH)
    score_scale = 1.0 / math.sqrt(DH)

    def one_block(query_block):
        scores = (
            jnp.einsum("qgd,kgd->gqk", query_block, key_split, preferred_element_type=F32)
            * score_scale
        )
        row_max = jnp.max(scores, axis=2, keepdims=True)
        probs = jnp.exp(scores - row_max)
        totals = jnp.sum(probs, axis=2, keepdims=True)
        weights = probs.astype(BF16)
        accumulated = jnp.einsum(
            "gqk,kgd->gqd", weights, value_split, preferred_element_type=F32
        )
        attended = accumulated / totals
        attended = jnp.transpose(attended, (1, 0, 2)).reshape(block_height, heads_here * DH)
        return attended.astype(BF16)

    outputs = lax.map(one_block, query_blocks)
    return outputs.reshape(query_count, heads_here * DH)


def seq_exchange(stacked, split, concat):
    return lax.all_to_all(stacked, "seq", split_axis=split, concat_axis=concat, tiled=True)


def run_model(queries, keys, values, shared):
    seq_count = lax.axis_size("seq")
    heads = queries.shape[1] // DH
    blocks = max(seq_count // heads, 1)
    parts = heads // max(heads // seq_count, 1)
    query_rows = seq_exchange(split_heads(queries, blocks, parts), 0, 1)[0]
    key_rows = seq_exchange(copy_heads(keys, blocks, parts), 0, 1)[0]
    value_rows = seq_exchange(copy_heads(values, blocks, parts), 0, 1)[0]
    if shared:
        key_rows = lax.all_gather(key_rows, "head", axis=0, tiled=True)
        value_rows = lax.all_gather(value_rows, "head", axis=0, tiled=True)
    out = attend(query_rows, key_rows, value_rows)
    return join_heads(seq_exchange(out[None], 1, 0), blocks, parts)


def general_shards(bq, bk, bv, sq, sk, sv, br, sr, guidance):
    big_attention = run_model(bq, bk, bv, False)
    big_partial = jnp.dot(big_attention, br, preferred_element_type=F32)
    small_attention = run_model(sq, sk, sv, True)
    small_latent = jnp.dot(small_attention, sr, preferred_element_type=F32)
    weight_value = guidance[0]
    core_index = lax.axis_index("head")
    placed = lax.dynamic_update_slice(
        jnp.zeros_like(big_partial),
        small_latent,
        (core_index * small_latent.shape[0], jnp.zeros((), jnp.int32)),
    )
    blended = lax.psum((1.0 + weight_value) * big_partial - weight_value * placed, "head")
    return blended.reshape(blended.shape[0] // 2, 2 * blended.shape[1])


def solution(mesh):
    placed = (
        P(("groups", "seq"), "head"),
        P(("groups", "seq"), "head"),
        P(("groups", "seq"), "head"),
        P(("groups", "seq", "head"), None),
        P(("groups", "seq", "head"), None),
        P(("groups", "seq", "head"), None),
        P("head", None),
        P(),
        P("groups"),
    )

    def whole(*arrays):
        fits = fits_exchange(mesh, arrays[0], arrays[3], arrays[6])
        return jax.shard_map(
            exchange_shards if fits else general_shards,
            mesh=mesh,
            in_specs=placed,
            out_specs=P(("groups", "seq"), None),
            check_vma=False,
        )(*arrays)

    return whole
```

```python
import functools
import math

import jax
import jax.numpy as jnp
from jax import lax
from jax.experimental import pallas as pl
from jax.experimental.pallas import tpu as pltpu
from jax.sharding import PartitionSpec as P

DH = 128
BF16 = jnp.bfloat16
F32 = jnp.float32
VMEM = pl.BlockSpec(memory_space=pltpu.VMEM)
HBM = pl.BlockSpec(memory_space=pltpu.HBM)
SMEM = pl.BlockSpec(memory_space=pltpu.SMEM)
NT = (((1,), (1,)), ((), ()))


def near_count(n):
    return n // 2


def hop_order(n):
    return [0] + [2, 4, 1, 7, 3, 5, 6] if n == 8 else list(range(n))


def row_layout(group, small_group, tokens, small_tokens):
    rows = {}
    at = 0
    for name, count in (
        ("k", group * tokens),
        ("vr", group // 2 * tokens),
        ("sk", small_group * small_tokens),
        ("svr", small_tokens),
        ("far", 0),
        ("q", group * tokens),
        ("sq", small_group * small_tokens),
        ("near", 0),
    ):
        rows[name] = at
        at += count
    return rows


def pack_kernel(n, near, group, small_group, rows, *refs):
    sources, outs, held, done = refs[:8], refs[8 : 8 + n], refs[8 + n : 16 + n], refs[16 + n]
    copies = [pltpu.make_async_copy(sources[i], held[i], done.at[i]) for i in range(8)]
    for copy in copies:
        copy.start()
    sv, sr, bv, br, sk, sq, bk, bq = held
    tokens, small_tokens = bk.shape[0], sk.shape[0]
    me = lax.axis_index("seq")

    def columns(j, heads, g):
        first = jnp.bitwise_xor(me, j) % near * heads + g
        return pl.ds(pl.multiple_of(first * DH, DH), DH)

    def put(j, row, value):
        for k in range(j, n, near):
            outs[k][pl.ds(row, value.shape[0]), :] = value

    def project(values, readout, heads, j, g):
        first = jnp.bitwise_xor(me, j) % near * heads + g
        cols = pl.ds(pl.multiple_of(first * DH, DH), 2 * DH)
        pair = readout[:, cols]
        none = jnp.zeros((readout.shape[0], DH), BF16)
        left = jnp.concatenate([pair[:, :DH], none], axis=1)
        right = jnp.concatenate([none, pair[:, DH:]], axis=1)
        both = jnp.concatenate([left, right], axis=0)
        out = lax.dot_general(values[:, cols], both, NT, preferred_element_type=F32)
        return out.astype(BF16)

    copies[0].wait()
    copies[1].wait()
    for j in range(near):
        put(j, rows["svr"], project(sv, sr, small_group, j, 0))
    copies[2].wait()
    copies[3].wait()
    for j in range(near):
        for g in range(0, group, 2):
            put(j, rows["vr"] + g // 2 * tokens, project(bv, br, group, j, g))
    copies[4].wait()
    copies[5].wait()
    for j in range(near):
        for g in range(small_group):
            cols = columns(j, small_group, g)
            put(j, rows["sk"] + g * small_tokens, sk[:, cols])
            outs[j][pl.ds(rows["sq"] + g * small_tokens, small_tokens), :] = sq[:, cols]
    copies[6].wait()
    copies[7].wait()
    for j in range(near):
        for g in range(group):
            cols = columns(j, group, g)
            put(j, rows["k"] + g * tokens, bk[:, cols])
            outs[j][pl.ds(rows["q"] + g * tokens, tokens), :] = bq[:, cols]


def gather_small_kernel(order, near, rows, *refs):
    n = len(order)
    blocks, (guidance, out, weight) = refs[:n], refs[n:]
    weight[:, :] = jnp.full(weight.shape, guidance[0], F32)
    at = 0
    for block, k in zip(blocks, order):
        parts = [(rows["sk"], rows["far"])] + ([(rows["sq"], rows["near"])] if k < near else [])
        for first, last in parts:
            out[pl.ds(at, last - first), :] = block[pl.ds(first, last - first), :]
            at += last - first


def attend_heads(heads, lat):
    scale = math.log2(math.e) / math.sqrt(DH)
    scores = [
        lax.dot_general(keys, queries, NT, preferred_element_type=F32)
        for queries, keys, _ in heads
    ]
    weights, totals = [], []
    for x in scores:
        probs = jnp.exp2((x - jnp.max(x, axis=0, keepdims=True)) * scale)
        totals.append(jnp.sum(probs, axis=0, keepdims=True))
        weights.append(probs.astype(BF16))
    out = None
    for (_, _, values), weight, total in zip(heads, weights, totals):
        part = jnp.dot(values, weight, preferred_element_type=F32) / total
        out = part if out is None else out + part
    return out


def big_kernel(order, near, group, tokens, lat, rows, *refs):
    n = len(order)
    blocks, out = refs[:n], refs[n]
    here = [b for b, k in zip(blocks, order) if k < near]
    read = lambda some, first: jnp.concatenate(
        [b[pl.ds(first, tokens), :] for b in some], axis=0
    )
    values = [read(blocks, rows["vr"] + p * tokens).T for p in range(group // 2)]
    out[:, :] = attend_heads(
        [
            (
                read(here, rows["q"] + g * tokens),
                read(blocks, rows["k"] + g * tokens),
                values[g // 2][g % 2 * lat : (g % 2 + 1) * lat, :],
            )
            for g in range(group)
        ],
        lat,
    )


def small_kernel(order, near, small_group, tokens, count, lat, rows, *refs):
    n = len(order)
    blocks, theirs, out = refs[:n], refs[n], refs[n + 1]
    first_core = lax.axis_index("head") == 0
    at = 0
    found = {name: [] for name in ("sk", "svr", "sq")}
    for block, k in zip(blocks, order):
        for name, size in (
            ("sk", small_group * count),
            ("svr", count),
            ("sq", small_group * count),
        ):
            if name == "sq" and k >= near:
                continue
            own = block[pl.ds(rows[name], size), :]
            found[name].append((own, theirs[pl.ds(at, size), :]))
            at += size
    values = jnp.concatenate([p[side] for side in (0, 1) for p in found["svr"]], axis=0).T
    heads = []
    for g in range(small_group):
        head = slice(g * count, (g + 1) * count)
        keys = [p[side][head] for side in (0, 1) for p in found["sk"]]
        queries = []
        for own, other in found["sq"]:
            queries.append(jnp.where(first_core, own[head], other[head]))
            queries.append(jnp.where(first_core, other[head], own[head]))
        heads.append(
            (
                jnp.concatenate(queries, axis=0),
                jnp.concatenate(keys, axis=0),
                values[g * lat : (g + 1) * lat, :],
            )
        )
    out[:, :] = attend_heads(heads, lat)


def blend_kernel(near, tokens, big, other_big, small, weight, *refs):
    outs, latent = refs[:near], refs[near]
    lat, width = big.shape
    scale = weight[:1, :1]
    blended = (1.0 + scale) * (big[:, :] + other_big[:, :]) - scale * small[:, :]
    latent[:, :lat] = blended.T
    for i in range(near):
        even = latent[pl.ds(i * tokens, tokens // 2, stride=2), :lat]
        odd = latent[pl.ds(i * tokens + 1, tokens // 2, stride=2), :lat]
        outs[i][:, :] = jnp.concatenate([even, odd], axis=1)


def sum_kernel(*refs):
    total = refs[0][:, :]
    for x in refs[1:-1]:
        total = total + x[:, :]
    refs[-1][:, :] = total


def call(kernel, out_shape, operands, specs=None, scratch=(), cost=None):
    single = not isinstance(out_shape, (list, tuple))
    return pl.pallas_call(
        kernel,
        out_shape=out_shape,
        in_specs=specs if specs is not None else [VMEM] * len(operands),
        out_specs=VMEM if single else [VMEM] * len(out_shape),
        scratch_shapes=list(scratch),
        cost_estimate=cost,
        compiler_params=pltpu.CompilerParams(vmem_limit_bytes=16 * 2**20),
    )(*operands)


def exchange_shards(bq, bk, bv, sq, sk, sv, br, sr, guidance):
    n, cores = lax.axis_size("seq"), lax.axis_size("head")
    near = near_count(n)
    order = hop_order(n)
    tokens, count = bq.shape[0], sq.shape[0]
    group, small_group = bq.shape[1] // DH // near, sq.shape[1] // DH // near
    lat = br.shape[1]
    rows = row_layout(group, small_group, tokens, count)
    shape = lambda *dims, dtype=BF16: jax.ShapeDtypeStruct(dims, dtype)
    sources = [
        pltpu.with_memory_space_constraint(a, pltpu.HBM)
        for a in (sv, sr.T, bv, br.T, sk, sq, bk, bq)
    ]
    sent = call(
        functools.partial(pack_kernel, n, near, group, small_group, rows),
        [shape(rows["near" if k < near else "far"], DH) for k in range(n)],
        sources,
        specs=[HBM] * len(sources),
        scratch=[pltpu.VMEM(a.shape, a.dtype) for a in sources]
        + [pltpu.SemaphoreType.DMA((len(sources),))],
    )
    blocks = [sent[0]]
    for k in order[1:]:
        blocks.append(lax.ppermute(sent[k], "seq", [(j, j ^ k) for j in range(n)]))
    ours, weight = call(
        functools.partial(gather_small_kernel, order, near, rows),
        [
            shape(n * (rows["far"] - rows["sk"]) + near * (rows["near"] - rows["sq"]), DH),
            shape(8, DH, dtype=F32),
        ],
        (*blocks, guidance),
        specs=[VMEM] * n + [SMEM],
    )
    swap = lambda a: lax.ppermute(a, "head", [(c, c ^ 1) for c in range(cores)])
    theirs = swap(ours)
    big = call(
        functools.partial(big_kernel, order, near, group, tokens, lat, rows),
        shape(lat, near * tokens, dtype=F32),
        blocks,
        cost=pl.CostEstimate(flops=10**9, bytes_accessed=10**6, transcendentals=10**5),
    )
    other_big = swap(big)
    small = call(
        functools.partial(small_kernel, order, near, small_group, tokens, count, lat, rows),
        shape(lat, near * tokens, dtype=F32),
        (*blocks, theirs),
        cost=pl.CostEstimate(flops=10**9, bytes_accessed=10**6, transcendentals=10**5),
    )
    hops = [k for k in order if k < near]
    terms = call(
        functools.partial(blend_kernel, near, tokens),
        [shape(tokens // 2, 2 * lat, dtype=F32)] * near,
        (big, other_big, small, weight),
        scratch=[pltpu.VMEM((near * tokens, DH), F32)],
    )
    sums = [terms[0]]
    for i in (3, 2, 1):
        sums.append(lax.ppermute(terms[i], "seq", [(j, j ^ hops[i]) for j in range(n)]))
    return call(sum_kernel, shape(tokens // 2, 2 * lat, dtype=F32), sums)


def fits_exchange(mesh, bq, sq, br):
    groups, n, cores = mesh.shape["groups"], mesh.shape["seq"], mesh.shape["head"]
    near = near_count(n)
    tokens = bq.shape[0] // (groups * n)
    count = sq.shape[0] // (groups * n * cores)
    big_heads, small_heads = bq.shape[1] // DH // cores, sq.shape[1] // DH
    return (
        cores == 2
        and n & (n - 1) == 0
        and near >= 1
        and small_heads == near * cores
        and big_heads % (2 * near) == 0
        and 2 * br.shape[1] == DH
        and count % 16 == 0
        and n * tokens <= 1024
    )


def split_heads(matrix, blocks, parts):
    rows_here, columns = matrix.shape
    shaped = matrix.reshape(blocks, rows_here // blocks, parts, columns // parts)
    shaped = jnp.transpose(shaped, (0, 2, 1, 3))
    return shaped.reshape(blocks * parts, rows_here // blocks, columns // parts)


def copy_heads(matrix, blocks, parts):
    rows_here, columns = matrix.shape
    shaped = jnp.transpose(matrix.reshape(rows_here, parts, columns // parts), (1, 0, 2))
    shaped = jnp.broadcast_to(shaped[None], (blocks, parts, rows_here, columns // parts))
    return shaped.reshape(blocks * parts, rows_here, columns // parts)


def join_heads(stacked, blocks, parts):
    pieces, rows_here, columns = stacked.shape
    shaped = stacked.reshape(blocks, parts, rows_here, columns)
    shaped = jnp.transpose(shaped, (0, 2, 1, 3))
    return shaped.reshape(blocks * rows_here, parts * columns)


def attend(query_rows, key_rows, value_rows):
    query_count = query_rows.shape[0]
    heads_here = query_rows.shape[1] // DH
    key_count = key_rows.shape[0]
    block_height = math.gcd(query_count, 256)
    block_count = query_count // block_height
    query_blocks = query_rows.reshape(block_count, block_height, heads_here, DH)
    key_split = key_rows.reshape(key_count, heads_here, DH)
    value_split = value_rows.reshape(key_count, heads_here, DH)
    score_scale = 1.0 / math.sqrt(DH)

    def one_block(query_block):
        scores = (
            jnp.einsum("qgd,kgd->gqk", query_block, key_split, preferred_element_type=F32)
            * score_scale
        )
        row_max = jnp.max(scores, axis=2, keepdims=True)
        probs = jnp.exp(scores - row_max)
        totals = jnp.sum(probs, axis=2, keepdims=True)
        weights = probs.astype(BF16)
        accumulated = jnp.einsum(
            "gqk,kgd->gqd", weights, value_split, preferred_element_type=F32
        )
        attended = accumulated / totals
        attended = jnp.transpose(attended, (1, 0, 2)).reshape(block_height, heads_here * DH)
        return attended.astype(BF16)

    outputs = lax.map(one_block, query_blocks)
    return outputs.reshape(query_count, heads_here * DH)


def seq_exchange(stacked, split, concat):
    return lax.all_to_all(stacked, "seq", split_axis=split, concat_axis=concat, tiled=True)


def run_model(queries, keys, values, shared):
    seq_count = lax.axis_size("seq")
    heads = queries.shape[1] // DH
    blocks = max(seq_count // heads, 1)
    parts = heads // max(heads // seq_count, 1)
    query_rows = seq_exchange(split_heads(queries, blocks, parts), 0, 1)[0]
    key_rows = seq_exchange(copy_heads(keys, blocks, parts), 0, 1)[0]
    value_rows = seq_exchange(copy_heads(values, blocks, parts), 0, 1)[0]
    if shared:
        key_rows = lax.all_gather(key_rows, "head", axis=0, tiled=True)
        value_rows = lax.all_gather(value_rows, "head", axis=0, tiled=True)
    out = attend(query_rows, key_rows, value_rows)
    return join_heads(seq_exchange(out[None], 1, 0), blocks, parts)


def general_shards(bq, bk, bv, sq, sk, sv, br, sr, guidance):
    big_attention = run_model(bq, bk, bv, False)
    big_partial = jnp.dot(big_attention, br, preferred_element_type=F32)
    small_attention = run_model(sq, sk, sv, True)
    small_latent = jnp.dot(small_attention, sr, preferred_element_type=F32)
    weight_value = guidance[0]
    core_index = lax.axis_index("head")
    placed = lax.dynamic_update_slice(
        jnp.zeros_like(big_partial),
        small_latent,
        (core_index * small_latent.shape[0], jnp.zeros((), jnp.int32)),
    )
    blended = lax.psum((1.0 + weight_value) * big_partial - weight_value * placed, "head")
    return blended.reshape(blended.shape[0] // 2, 2 * blended.shape[1])


def solution(mesh):
    placed = (
        P(("groups", "seq"), "head"),
        P(("groups", "seq"), "head"),
        P(("groups", "seq"), "head"),
        P(("groups", "seq", "head"), None),
        P(("groups", "seq", "head"), None),
        P(("groups", "seq", "head"), None),
        P("head", None),
        P(),
        P("groups"),
    )

    def whole(*arrays):
        fits = fits_exchange(mesh, arrays[0], arrays[3], arrays[6])
        return jax.shard_map(
            exchange_shards if fits else general_shards,
            mesh=mesh,
            in_specs=placed,
            out_specs=P(("groups", "seq"), None),
            check_vma=False,
        )(*arrays)

    return whole
```

```python
import functools
import math

import jax
import jax.numpy as jnp
from jax import lax
from jax.experimental import pallas as pl
from jax.experimental.pallas import tpu as pltpu
from jax.sharding import PartitionSpec as P

DH = 128
BF16 = jnp.bfloat16
F32 = jnp.float32
VMEM = pl.BlockSpec(memory_space=pltpu.VMEM)
HBM = pl.BlockSpec(memory_space=pltpu.HBM)
SMEM = pl.BlockSpec(memory_space=pltpu.SMEM)
NT = (((1,), (1,)), ((), ()))


def near_count(n):
    return n // 2


def hop_order(n):
    return [0] + [2, 4, 1, 7, 3, 5, 6] if n == 8 else list(range(n))


def row_layout(group, small_group, tokens, small_tokens):
    rows = {}
    at = 0
    for name, count in (
        ("k", group * tokens),
        ("vr", group // 2 * tokens),
        ("sk", small_group * small_tokens),
        ("svr", small_tokens),
        ("far", 0),
        ("q", group * tokens),
        ("sq", small_group * small_tokens),
        ("near", 0),
    ):
        rows[name] = at
        at += count
    return rows


def pack_kernel(n, near, group, small_group, rows, *refs):
    sources, outs, held, done = refs[:8], refs[8 : 8 + n], refs[8 + n : 16 + n], refs[16 + n]
    copies = [pltpu.make_async_copy(sources[i], held[i], done.at[i]) for i in range(8)]
    for copy in copies:
        copy.start()
    sv, sr, bv, br, sk, sq, bk, bq = held
    tokens, small_tokens = bk.shape[0], sk.shape[0]
    me = lax.axis_index("seq")

    def columns(j, heads, g):
        first = jnp.bitwise_xor(me, j) % near * heads + g
        return pl.ds(pl.multiple_of(first * DH, DH), DH)

    def put(j, row, value):
        for k in range(j, n, near):
            outs[k][pl.ds(row, value.shape[0]), :] = value

    def project(values, readout, heads, j, g):
        first = jnp.bitwise_xor(me, j) % near * heads + g
        cols = pl.ds(pl.multiple_of(first * DH, DH), 2 * DH)
        pair = readout[:, cols]
        none = jnp.zeros((readout.shape[0], DH), BF16)
        left = jnp.concatenate([pair[:, :DH], none], axis=1)
        right = jnp.concatenate([none, pair[:, DH:]], axis=1)
        both = jnp.concatenate([left, right], axis=0)
        out = lax.dot_general(values[:, cols], both, NT, preferred_element_type=F32)
        return out.astype(BF16)

    copies[0].wait()
    copies[1].wait()
    for j in range(near):
        put(j, rows["svr"], project(sv, sr, small_group, j, 0))
    copies[2].wait()
    copies[3].wait()
    for j in range(near):
        for g in range(0, group, 2):
            put(j, rows["vr"] + g // 2 * tokens, project(bv, br, group, j, g))
    copies[4].wait()
    copies[5].wait()
    for j in range(near):
        for g in range(small_group):
            cols = columns(j, small_group, g)
            put(j, rows["sk"] + g * small_tokens, sk[:, cols])
            outs[j][pl.ds(rows["sq"] + g * small_tokens, small_tokens), :] = sq[:, cols]
    copies[6].wait()
    copies[7].wait()
    for j in range(near):
        for g in range(group):
            cols = columns(j, group, g)
            put(j, rows["k"] + g * tokens, bk[:, cols])
            outs[j][pl.ds(rows["q"] + g * tokens, tokens), :] = bq[:, cols]


def gather_small_kernel(order, near, rows, *refs):
    n = len(order)
    blocks, (guidance, out, weight) = refs[:n], refs[n:]
    weight[:, :] = jnp.full(weight.shape, guidance[0], F32)
    at = 0
    for block, k in zip(blocks, order):
        parts = [(rows["sk"], rows["far"])] + ([(rows["sq"], rows["near"])] if k < near else [])
        for first, last in parts:
            out[pl.ds(at, last - first), :] = block[pl.ds(first, last - first), :]
            at += last - first


def attend_heads(heads, lat):
    scale = math.log2(math.e) / math.sqrt(DH)
    scores = [
        lax.dot_general(keys, queries, NT, preferred_element_type=F32)
        for queries, keys, _ in heads
    ]
    weights, totals = [], []
    for x in scores:
        probs = jnp.exp2((x - jnp.max(x, axis=0, keepdims=True)) * scale)
        totals.append(jnp.sum(probs, axis=0, keepdims=True))
        weights.append(probs.astype(BF16))
    out = None
    for (_, _, values), weight, total in zip(heads, weights, totals):
        part = jnp.dot(values, weight, preferred_element_type=F32) / total
        out = part if out is None else out + part
    return out


def big_kernel(order, near, group, tokens, lat, rows, *refs):
    n = len(order)
    blocks, out = refs[:n], refs[n]
    here = [b for b, k in zip(blocks, order) if k < near]
    read = lambda some, first: jnp.concatenate(
        [b[pl.ds(first, tokens), :] for b in some], axis=0
    )
    values = [read(blocks, rows["vr"] + p * tokens).T for p in range(group // 2)]
    out[:, :] = attend_heads(
        [
            (
                read(here, rows["q"] + g * tokens),
                read(blocks, rows["k"] + g * tokens),
                values[g // 2][g % 2 * lat : (g % 2 + 1) * lat, :],
            )
            for g in range(group)
        ],
        lat,
    )


def small_kernel(order, near, small_group, tokens, count, lat, rows, *refs):
    n = len(order)
    blocks, theirs, out = refs[:n], refs[n], refs[n + 1]
    first_core = lax.axis_index("head") == 0
    at = 0
    found = {name: [] for name in ("sk", "svr", "sq")}
    for block, k in zip(blocks, order):
        for name, size in (
            ("sk", small_group * count),
            ("svr", count),
            ("sq", small_group * count),
        ):
            if name == "sq" and k >= near:
                continue
            own = block[pl.ds(rows[name], size), :]
            found[name].append((own, theirs[pl.ds(at, size), :]))
            at += size
    values = jnp.concatenate([p[side] for side in (0, 1) for p in found["svr"]], axis=0).T
    heads = []
    for g in range(small_group):
        head = slice(g * count, (g + 1) * count)
        keys = [p[side][head] for side in (0, 1) for p in found["sk"]]
        queries = []
        for own, other in found["sq"]:
            queries.append(jnp.where(first_core, own[head], other[head]))
            queries.append(jnp.where(first_core, other[head], own[head]))
        heads.append(
            (
                jnp.concatenate(queries, axis=0),
                jnp.concatenate(keys, axis=0),
                values[g * lat : (g + 1) * lat, :],
            )
        )
    out[:, :] = attend_heads(heads, lat)


def blend_kernel(near, tokens, big, other_big, small, weight, *refs):
    outs, latent = refs[:near], refs[near]
    lat, width = big.shape
    scale = weight[:1, :1]
    blended = (1.0 + scale) * (big[:, :] + other_big[:, :]) - scale * small[:, :]
    latent[:, :lat] = blended.T
    for i in range(near):
        even = latent[pl.ds(i * tokens, tokens // 2, stride=2), :lat]
        odd = latent[pl.ds(i * tokens + 1, tokens // 2, stride=2), :lat]
        outs[i][:, :] = jnp.concatenate([even, odd], axis=1)


def sum_kernel(*refs):
    total = refs[0][:, :]
    for x in refs[1:-1]:
        total = total + x[:, :]
    refs[-1][:, :] = total


def call(kernel, out_shape, operands, specs=None, scratch=(), cost=None):
    single = not isinstance(out_shape, (list, tuple))
    return pl.pallas_call(
        kernel,
        out_shape=out_shape,
        in_specs=specs if specs is not None else [VMEM] * len(operands),
        out_specs=VMEM if single else [VMEM] * len(out_shape),
        scratch_shapes=list(scratch),
        cost_estimate=cost,
        compiler_params=pltpu.CompilerParams(vmem_limit_bytes=16 * 2**20),
    )(*operands)


def exchange_shards(bq, bk, bv, sq, sk, sv, br, sr, guidance):
    n, cores = lax.axis_size("seq"), lax.axis_size("head")
    near = near_count(n)
    order = hop_order(n)
    tokens, count = bq.shape[0], sq.shape[0]
    group, small_group = bq.shape[1] // DH // near, sq.shape[1] // DH // near
    lat = br.shape[1]
    rows = row_layout(group, small_group, tokens, count)
    shape = lambda *dims, dtype=BF16: jax.ShapeDtypeStruct(dims, dtype)
    sources = [
        pltpu.with_memory_space_constraint(a, pltpu.HBM)
        for a in (sv, sr.T, bv, br.T, sk, sq, bk, bq)
    ]
    sent = call(
        functools.partial(pack_kernel, n, near, group, small_group, rows),
        [shape(rows["near" if k < near else "far"], DH) for k in range(n)],
        sources,
        specs=[HBM] * len(sources),
        scratch=[pltpu.VMEM(a.shape, a.dtype) for a in sources]
        + [pltpu.SemaphoreType.DMA((len(sources),))],
    )
    blocks = [sent[0]]
    for k in order[1:]:
        blocks.append(lax.ppermute(sent[k], "seq", [(j, j ^ k) for j in range(n)]))
    ours, weight = call(
        functools.partial(gather_small_kernel, order, near, rows),
        [
            shape(n * (rows["far"] - rows["sk"]) + near * (rows["near"] - rows["sq"]), DH),
            shape(8, DH, dtype=F32),
        ],
        (*blocks, guidance),
        specs=[VMEM] * n + [SMEM],
    )
    swap = lambda a: lax.ppermute(a, "head", [(c, c ^ 1) for c in range(cores)])
    theirs = swap(ours)
    big = call(
        functools.partial(big_kernel, order, near, group, tokens, lat, rows),
        shape(lat, near * tokens, dtype=F32),
        blocks,
        cost=pl.CostEstimate(flops=10**9, bytes_accessed=10**6, transcendentals=10**5),
    )
    other_big = swap(big)
    small = call(
        functools.partial(small_kernel, order, near, small_group, tokens, count, lat, rows),
        shape(lat, near * tokens, dtype=F32),
        (*blocks, theirs),
        cost=pl.CostEstimate(flops=10**9, bytes_accessed=10**6, transcendentals=10**5),
    )
    hops = [k for k in order if k < near]
    terms = call(
        functools.partial(blend_kernel, near, tokens),
        [shape(tokens // 2, 2 * lat, dtype=F32)] * near,
        (big, other_big, small, weight),
        scratch=[pltpu.VMEM((near * tokens, DH), F32)],
    )
    sums = [terms[0]]
    for i in (3, 2, 1):
        pairs = [(j * cores + c, (j ^ hops[i]) * cores + (c ^ 1)) for j in range(n) for c in range(cores)]
        sums.append(lax.ppermute(terms[i], ("seq", "head"), pairs))
    return call(sum_kernel, shape(tokens // 2, 2 * lat, dtype=F32), sums)


def fits_exchange(mesh, bq, sq, br):
    groups, n, cores = mesh.shape["groups"], mesh.shape["seq"], mesh.shape["head"]
    near = near_count(n)
    tokens = bq.shape[0] // (groups * n)
    count = sq.shape[0] // (groups * n * cores)
    big_heads, small_heads = bq.shape[1] // DH // cores, sq.shape[1] // DH
    return (
        cores == 2
        and n & (n - 1) == 0
        and near >= 1
        and small_heads == near * cores
        and big_heads % (2 * near) == 0
        and 2 * br.shape[1] == DH
        and count % 16 == 0
        and n * tokens <= 1024
    )


def split_heads(matrix, blocks, parts):
    rows_here, columns = matrix.shape
    shaped = matrix.reshape(blocks, rows_here // blocks, parts, columns // parts)
    shaped = jnp.transpose(shaped, (0, 2, 1, 3))
    return shaped.reshape(blocks * parts, rows_here // blocks, columns // parts)


def copy_heads(matrix, blocks, parts):
    rows_here, columns = matrix.shape
    shaped = jnp.transpose(matrix.reshape(rows_here, parts, columns // parts), (1, 0, 2))
    shaped = jnp.broadcast_to(shaped[None], (blocks, parts, rows_here, columns // parts))
    return shaped.reshape(blocks * parts, rows_here, columns // parts)


def join_heads(stacked, blocks, parts):
    pieces, rows_here, columns = stacked.shape
    shaped = stacked.reshape(blocks, parts, rows_here, columns)
    shaped = jnp.transpose(shaped, (0, 2, 1, 3))
    return shaped.reshape(blocks * rows_here, parts * columns)


def attend(query_rows, key_rows, value_rows):
    query_count = query_rows.shape[0]
    heads_here = query_rows.shape[1] // DH
    key_count = key_rows.shape[0]
    block_height = math.gcd(query_count, 256)
    block_count = query_count // block_height
    query_blocks = query_rows.reshape(block_count, block_height, heads_here, DH)
    key_split = key_rows.reshape(key_count, heads_here, DH)
    value_split = value_rows.reshape(key_count, heads_here, DH)
    score_scale = 1.0 / math.sqrt(DH)

    def one_block(query_block):
        scores = (
            jnp.einsum("qgd,kgd->gqk", query_block, key_split, preferred_element_type=F32)
            * score_scale
        )
        row_max = jnp.max(scores, axis=2, keepdims=True)
        probs = jnp.exp(scores - row_max)
        totals = jnp.sum(probs, axis=2, keepdims=True)
        weights = probs.astype(BF16)
        accumulated = jnp.einsum(
            "gqk,kgd->gqd", weights, value_split, preferred_element_type=F32
        )
        attended = accumulated / totals
        attended = jnp.transpose(attended, (1, 0, 2)).reshape(block_height, heads_here * DH)
        return attended.astype(BF16)

    outputs = lax.map(one_block, query_blocks)
    return outputs.reshape(query_count, heads_here * DH)


def seq_exchange(stacked, split, concat):
    return lax.all_to_all(stacked, "seq", split_axis=split, concat_axis=concat, tiled=True)


def run_model(queries, keys, values, shared):
    seq_count = lax.axis_size("seq")
    heads = queries.shape[1] // DH
    blocks = max(seq_count // heads, 1)
    parts = heads // max(heads // seq_count, 1)
    query_rows = seq_exchange(split_heads(queries, blocks, parts), 0, 1)[0]
    key_rows = seq_exchange(copy_heads(keys, blocks, parts), 0, 1)[0]
    value_rows = seq_exchange(copy_heads(values, blocks, parts), 0, 1)[0]
    if shared:
        key_rows = lax.all_gather(key_rows, "head", axis=0, tiled=True)
        value_rows = lax.all_gather(value_rows, "head", axis=0, tiled=True)
    out = attend(query_rows, key_rows, value_rows)
    return join_heads(seq_exchange(out[None], 1, 0), blocks, parts)


def general_shards(bq, bk, bv, sq, sk, sv, br, sr, guidance):
    big_attention = run_model(bq, bk, bv, False)
    big_partial = jnp.dot(big_attention, br, preferred_element_type=F32)
    small_attention = run_model(sq, sk, sv, True)
    small_latent = jnp.dot(small_attention, sr, preferred_element_type=F32)
    weight_value = guidance[0]
    core_index = lax.axis_index("head")
    placed = lax.dynamic_update_slice(
        jnp.zeros_like(big_partial),
        small_latent,
        (core_index * small_latent.shape[0], jnp.zeros((), jnp.int32)),
    )
    blended = lax.psum((1.0 + weight_value) * big_partial - weight_value * placed, "head")
    return blended.reshape(blended.shape[0] // 2, 2 * blended.shape[1])


def solution(mesh):
    placed = (
        P(("groups", "seq"), "head"),
        P(("groups", "seq"), "head"),
        P(("groups", "seq"), "head"),
        P(("groups", "seq", "head"), None),
        P(("groups", "seq", "head"), None),
        P(("groups", "seq", "head"), None),
        P("head", None),
        P(),
        P("groups"),
    )

    def whole(*arrays):
        fits = fits_exchange(mesh, arrays[0], arrays[3], arrays[6])
        return jax.shard_map(
            exchange_shards if fits else general_shards,
            mesh=mesh,
            in_specs=placed,
            out_specs=P(("groups", "seq"), None),
            check_vma=False,
        )(*arrays)

    return whole
```

```python
import functools
import math

import jax
import jax.numpy as jnp
from jax import lax
from jax.experimental import pallas as pl
from jax.experimental.pallas import tpu as pltpu
from jax.sharding import PartitionSpec as P

DH = 128
BF16 = jnp.bfloat16
F32 = jnp.float32
VMEM = pl.BlockSpec(memory_space=pltpu.VMEM)
HBM = pl.BlockSpec(memory_space=pltpu.HBM)
SMEM = pl.BlockSpec(memory_space=pltpu.SMEM)
NT = (((1,), (1,)), ((), ()))


def near_count(n):
    return n // 2


def hop_order(n):
    return [0] + [2, 4, 1, 7, 3, 5, 6] if n == 8 else list(range(n))


def row_layout(group, small_group, tokens, small_tokens):
    rows = {}
    at = 0
    for name, count in (
        ("k", group * tokens),
        ("vr", group // 2 * tokens),
        ("sk", small_group * small_tokens),
        ("svr", small_tokens),
        ("far", 0),
        ("q", group * tokens),
        ("sq", small_group * small_tokens),
        ("near", 0),
    ):
        rows[name] = at
        at += count
    return rows


def pack_kernel(n, near, group, small_group, rows, *refs):
    sources, outs, held, done = refs[:8], refs[8 : 8 + n], refs[8 + n : 16 + n], refs[16 + n]
    copies = [pltpu.make_async_copy(sources[i], held[i], done.at[i]) for i in range(8)]
    for copy in copies:
        copy.start()
    sv, sr, bv, br, sk, sq, bk, bq = held
    tokens, small_tokens = bk.shape[0], sk.shape[0]
    me = lax.axis_index("seq")

    def columns(j, heads, g):
        first = jnp.bitwise_xor(me, j) % near * heads + g
        return pl.ds(pl.multiple_of(first * DH, DH), DH)

    def put(j, row, value):
        for k in range(j, n, near):
            outs[k][pl.ds(row, value.shape[0]), :] = value

    def project(values, readout, heads, j, g):
        first = jnp.bitwise_xor(me, j) % near * heads + g
        cols = pl.ds(pl.multiple_of(first * DH, DH), 2 * DH)
        pair = readout[:, cols]
        none = jnp.zeros((readout.shape[0], DH), BF16)
        left = jnp.concatenate([pair[:, :DH], none], axis=1)
        right = jnp.concatenate([none, pair[:, DH:]], axis=1)
        both = jnp.concatenate([left, right], axis=0)
        out = lax.dot_general(values[:, cols], both, NT, preferred_element_type=F32)
        return out.astype(BF16)

    copies[0].wait()
    copies[1].wait()
    for j in range(near):
        put(j, rows["svr"], project(sv, sr, small_group, j, 0))
    copies[2].wait()
    copies[3].wait()
    for j in range(near):
        for g in range(0, group, 2):
            put(j, rows["vr"] + g // 2 * tokens, project(bv, br, group, j, g))
    copies[4].wait()
    copies[5].wait()
    for j in range(near):
        for g in range(small_group):
            cols = columns(j, small_group, g)
            put(j, rows["sk"] + g * small_tokens, sk[:, cols])
            outs[j][pl.ds(rows["sq"] + g * small_tokens, small_tokens), :] = sq[:, cols]
    copies[6].wait()
    copies[7].wait()
    for j in range(near):
        for g in range(group):
            cols = columns(j, group, g)
            put(j, rows["k"] + g * tokens, bk[:, cols])
            outs[j][pl.ds(rows["q"] + g * tokens, tokens), :] = bq[:, cols]


def gather_small_kernel(order, near, rows, *refs):
    n = len(order)
    blocks, (guidance, out, weight) = refs[:n], refs[n:]
    weight[:, :] = jnp.full(weight.shape, guidance[0], F32)
    at = 0
    for block, k in zip(blocks, order):
        parts = [(rows["sk"], rows["far"])] + ([(rows["sq"], rows["near"])] if k < near else [])
        for first, last in parts:
            out[pl.ds(at, last - first), :] = block[pl.ds(first, last - first), :]
            at += last - first


def attend_heads(heads, lat):
    scale = math.log2(math.e) / math.sqrt(DH)
    scores = [
        lax.dot_general(keys, queries, NT, preferred_element_type=F32)
        for queries, keys, _ in heads
    ]
    weights, totals = [], []
    for x in scores:
        probs = jnp.exp2((x - jnp.max(x, axis=0, keepdims=True)) * scale)
        totals.append(jnp.sum(probs, axis=0, keepdims=True))
        weights.append(probs.astype(BF16))
    out = None
    for (_, _, values), weight, total in zip(heads, weights, totals):
        part = jnp.dot(values, weight, preferred_element_type=F32) / total
        out = part if out is None else out + part
    return out


def big_kernel(order, near, group, tokens, lat, rows, *refs):
    n = len(order)
    blocks, out = refs[:n], refs[n]
    here = [b for b, k in zip(blocks, order) if k < near]
    read = lambda some, first: jnp.concatenate(
        [b[pl.ds(first, tokens), :] for b in some], axis=0
    )
    values = [read(blocks, rows["vr"] + p * tokens).T for p in range(group // 2)]
    out[:, :] = attend_heads(
        [
            (
                read(here, rows["q"] + g * tokens),
                read(blocks, rows["k"] + g * tokens),
                values[g // 2][g % 2 * lat : (g % 2 + 1) * lat, :],
            )
            for g in range(group)
        ],
        lat,
    )


def small_kernel(order, near, small_group, tokens, count, lat, rows, *refs):
    n = len(order)
    blocks, theirs, out = refs[:n], refs[n], refs[n + 1]
    first_core = lax.axis_index("head") == 0
    at = 0
    found = {name: [] for name in ("sk", "svr", "sq")}
    for block, k in zip(blocks, order):
        for name, size in (
            ("sk", small_group * count),
            ("svr", count),
            ("sq", small_group * count),
        ):
            if name == "sq" and k >= near:
                continue
            own = block[pl.ds(rows[name], size), :]
            found[name].append((own, theirs[pl.ds(at, size), :]))
            at += size
    values = jnp.concatenate([p[side] for side in (0, 1) for p in found["svr"]], axis=0).T
    heads = []
    for g in range(small_group):
        head = slice(g * count, (g + 1) * count)
        keys = [p[side][head] for side in (0, 1) for p in found["sk"]]
        queries = []
        for own, other in found["sq"]:
            queries.append(jnp.where(first_core, own[head], other[head]))
            queries.append(jnp.where(first_core, other[head], own[head]))
        heads.append(
            (
                jnp.concatenate(queries, axis=0),
                jnp.concatenate(keys, axis=0),
                values[g * lat : (g + 1) * lat, :],
            )
        )
    out[:, :] = attend_heads(heads, lat)


def blend_kernel(near, tokens, big, other_big, small, weight, *refs):
    outs, latent = refs[:near], refs[near]
    lat, width = big.shape
    scale = weight[:1, :1]
    blended = (1.0 + scale) * (big[:, :] + other_big[:, :]) - scale * small[:, :]
    latent[:width, :lat] = blended.T
    for i in range(near):
        even = latent[pl.ds(i * tokens, tokens // 2, stride=2), :lat]
        odd = latent[pl.ds(i * tokens + 1, tokens // 2, stride=2), :lat]
        outs[i][:, :] = jnp.concatenate([even, odd], axis=1)


def sum_kernel(*refs):
    total = refs[0][:, :]
    for x in refs[1:-1]:
        total = total + x[:, :]
    refs[-1][:, :] = total


def call(kernel, out_shape, operands, specs=None, scratch=(), cost=None):
    single = not isinstance(out_shape, (list, tuple))
    return pl.pallas_call(
        kernel,
        out_shape=out_shape,
        in_specs=specs if specs is not None else [VMEM] * len(operands),
        out_specs=VMEM if single else [VMEM] * len(out_shape),
        scratch_shapes=list(scratch),
        cost_estimate=cost,
        compiler_params=pltpu.CompilerParams(vmem_limit_bytes=16 * 2**20),
    )(*operands)


def exchange_shards(bq, bk, bv, sq, sk, sv, br, sr, guidance):
    n, cores = lax.axis_size("seq"), lax.axis_size("head")
    near = near_count(n)
    order = hop_order(n)
    tokens, count = bq.shape[0], sq.shape[0]
    group, small_group = bq.shape[1] // DH // near, sq.shape[1] // DH // near
    lat = br.shape[1]
    rows = row_layout(group, small_group, tokens, count)
    shape = lambda *dims, dtype=BF16: jax.ShapeDtypeStruct(dims, dtype)
    sources = [
        pltpu.with_memory_space_constraint(a, pltpu.HBM)
        for a in (sv, sr.T, bv, br.T, sk, sq, bk, bq)
    ]
    sent = call(
        functools.partial(pack_kernel, n, near, group, small_group, rows),
        [shape(rows["near" if k < near else "far"], DH) for k in range(n)],
        sources,
        specs=[HBM] * len(sources),
        scratch=[pltpu.VMEM(a.shape, a.dtype) for a in sources]
        + [pltpu.SemaphoreType.DMA((len(sources),))],
    )
    blocks = [sent[0]]
    for k in order[1:]:
        blocks.append(lax.ppermute(sent[k], "seq", [(j, j ^ k) for j in range(n)]))
    ours, weight = call(
        functools.partial(gather_small_kernel, order, near, rows),
        [
            shape(n * (rows["far"] - rows["sk"]) + near * (rows["near"] - rows["sq"]), DH),
            shape(8, DH, dtype=F32),
        ],
        (*blocks, guidance),
        specs=[VMEM] * n + [SMEM],
    )
    swap = lambda a: lax.ppermute(a, "head", [(c, c ^ 1) for c in range(cores)])
    theirs = swap(ours)
    big = call(
        functools.partial(big_kernel, order, near, group, tokens, lat, rows),
        shape(lat, near * tokens, dtype=F32),
        blocks,
        cost=pl.CostEstimate(flops=10**9, bytes_accessed=10**6, transcendentals=10**5),
    )
    other_big = swap(big)
    small = call(
        functools.partial(small_kernel, order, near, small_group, tokens, count, lat, rows),
        shape(lat, near * tokens, dtype=F32),
        (*blocks, theirs),
        cost=pl.CostEstimate(flops=10**9, bytes_accessed=10**6, transcendentals=10**5),
    )
    hops = [k for k in order if k < near]
    terms = call(
        functools.partial(blend_kernel, near, tokens),
        [shape(tokens // 2, 2 * lat, dtype=F32)] * near,
        (big, other_big, small, weight),
        scratch=[pltpu.VMEM((near * tokens + 8, DH), F32)],
    )
    sums = [terms[0]]
    for i in (3, 2, 1):
        pairs = [(j * cores + c, (j ^ hops[i]) * cores + (c ^ 1)) for j in range(n) for c in range(cores)]
        sums.append(lax.ppermute(terms[i], ("seq", "head"), pairs))
    return call(sum_kernel, shape(tokens // 2, 2 * lat, dtype=F32), sums)


def fits_exchange(mesh, bq, sq, br):
    groups, n, cores = mesh.shape["groups"], mesh.shape["seq"], mesh.shape["head"]
    near = near_count(n)
    tokens = bq.shape[0] // (groups * n)
    count = sq.shape[0] // (groups * n * cores)
    big_heads, small_heads = bq.shape[1] // DH // cores, sq.shape[1] // DH
    return (
        cores == 2
        and n & (n - 1) == 0
        and near >= 1
        and small_heads == near * cores
        and big_heads % (2 * near) == 0
        and 2 * br.shape[1] == DH
        and count % 16 == 0
        and n * tokens <= 1024
    )


def split_heads(matrix, blocks, parts):
    rows_here, columns = matrix.shape
    shaped = matrix.reshape(blocks, rows_here // blocks, parts, columns // parts)
    shaped = jnp.transpose(shaped, (0, 2, 1, 3))
    return shaped.reshape(blocks * parts, rows_here // blocks, columns // parts)


def copy_heads(matrix, blocks, parts):
    rows_here, columns = matrix.shape
    shaped = jnp.transpose(matrix.reshape(rows_here, parts, columns // parts), (1, 0, 2))
    shaped = jnp.broadcast_to(shaped[None], (blocks, parts, rows_here, columns // parts))
    return shaped.reshape(blocks * parts, rows_here, columns // parts)


def join_heads(stacked, blocks, parts):
    pieces, rows_here, columns = stacked.shape
    shaped = stacked.reshape(blocks, parts, rows_here, columns)
    shaped = jnp.transpose(shaped, (0, 2, 1, 3))
    return shaped.reshape(blocks * rows_here, parts * columns)


def attend(query_rows, key_rows, value_rows):
    query_count = query_rows.shape[0]
    heads_here = query_rows.shape[1] // DH
    key_count = key_rows.shape[0]
    block_height = math.gcd(query_count, 256)
    block_count = query_count // block_height
    query_blocks = query_rows.reshape(block_count, block_height, heads_here, DH)
    key_split = key_rows.reshape(key_count, heads_here, DH)
    value_split = value_rows.reshape(key_count, heads_here, DH)
    score_scale = 1.0 / math.sqrt(DH)

    def one_block(query_block):
        scores = (
            jnp.einsum("qgd,kgd->gqk", query_block, key_split, preferred_element_type=F32)
            * score_scale
        )
        row_max = jnp.max(scores, axis=2, keepdims=True)
        probs = jnp.exp(scores - row_max)
        totals = jnp.sum(probs, axis=2, keepdims=True)
        weights = probs.astype(BF16)
        accumulated = jnp.einsum(
            "gqk,kgd->gqd", weights, value_split, preferred_element_type=F32
        )
        attended = accumulated / totals
        attended = jnp.transpose(attended, (1, 0, 2)).reshape(block_height, heads_here * DH)
        return attended.astype(BF16)

    outputs = lax.map(one_block, query_blocks)
    return outputs.reshape(query_count, heads_here * DH)


def seq_exchange(stacked, split, concat):
    return lax.all_to_all(stacked, "seq", split_axis=split, concat_axis=concat, tiled=True)


def run_model(queries, keys, values, shared):
    seq_count = lax.axis_size("seq")
    heads = queries.shape[1] // DH
    blocks = max(seq_count // heads, 1)
    parts = heads // max(heads // seq_count, 1)
    query_rows = seq_exchange(split_heads(queries, blocks, parts), 0, 1)[0]
    key_rows = seq_exchange(copy_heads(keys, blocks, parts), 0, 1)[0]
    value_rows = seq_exchange(copy_heads(values, blocks, parts), 0, 1)[0]
    if shared:
        key_rows = lax.all_gather(key_rows, "head", axis=0, tiled=True)
        value_rows = lax.all_gather(value_rows, "head", axis=0, tiled=True)
    out = attend(query_rows, key_rows, value_rows)
    return join_heads(seq_exchange(out[None], 1, 0), blocks, parts)


def general_shards(bq, bk, bv, sq, sk, sv, br, sr, guidance):
    big_attention = run_model(bq, bk, bv, False)
    big_partial = jnp.dot(big_attention, br, preferred_element_type=F32)
    small_attention = run_model(sq, sk, sv, True)
    small_latent = jnp.dot(small_attention, sr, preferred_element_type=F32)
    weight_value = guidance[0]
    core_index = lax.axis_index("head")
    placed = lax.dynamic_update_slice(
        jnp.zeros_like(big_partial),
        small_latent,
        (core_index * small_latent.shape[0], jnp.zeros((), jnp.int32)),
    )
    blended = lax.psum((1.0 + weight_value) * big_partial - weight_value * placed, "head")
    return blended.reshape(blended.shape[0] // 2, 2 * blended.shape[1])


def solution(mesh):
    placed = (
        P(("groups", "seq"), "head"),
        P(("groups", "seq"), "head"),
        P(("groups", "seq"), "head"),
        P(("groups", "seq", "head"), None),
        P(("groups", "seq", "head"), None),
        P(("groups", "seq", "head"), None),
        P("head", None),
        P(),
        P("groups"),
    )

    def whole(*arrays):
        fits = fits_exchange(mesh, arrays[0], arrays[3], arrays[6])
        return jax.shard_map(
            exchange_shards if fits else general_shards,
            mesh=mesh,
            in_specs=placed,
            out_specs=P(("groups", "seq"), None),
            check_vma=False,
        )(*arrays)

    return whole
```

```python
import functools
import math

import jax
import jax.numpy as jnp
from jax import lax
from jax.experimental import pallas as pl
from jax.experimental.pallas import tpu as pltpu
from jax.sharding import PartitionSpec as P

DH = 128
BF16 = jnp.bfloat16
F32 = jnp.float32
VMEM = pl.BlockSpec(memory_space=pltpu.VMEM)
HBM = pl.BlockSpec(memory_space=pltpu.HBM)
SMEM = pl.BlockSpec(memory_space=pltpu.SMEM)
NT = (((1,), (1,)), ((), ()))


def near_count(n):
    return n // 2


def hop_order(n):
    return [0] + [6, 2, 5, 3, 7, 4, 1] if n == 8 else list(range(n))


def row_layout(group, small_group, tokens, small_tokens):
    rows = {}
    at = 0
    for name, count in (
        ("k", group * tokens),
        ("vr", group // 2 * tokens),
        ("sk", small_group * small_tokens),
        ("svr", small_tokens),
        ("far", 0),
        ("q", group * tokens),
        ("sq", small_group * small_tokens),
        ("near", 0),
    ):
        rows[name] = at
        at += count
    return rows


def pack_kernel(n, near, group, small_group, rows, *refs):
    sources, outs, held, done = refs[:8], refs[8 : 8 + n], refs[8 + n : 16 + n], refs[16 + n]
    copies = [pltpu.make_async_copy(sources[i], held[i], done.at[i]) for i in range(8)]
    for copy in copies:
        copy.start()
    sv, sr, bv, br, sk, sq, bk, bq = held
    tokens, small_tokens = bk.shape[0], sk.shape[0]
    me = lax.axis_index("seq")

    def columns(j, heads, g):
        first = jnp.bitwise_xor(me, j) % near * heads + g
        return pl.ds(pl.multiple_of(first * DH, DH), DH)

    def put(j, row, value):
        for k in range(j, n, near):
            outs[k][pl.ds(row, value.shape[0]), :] = value

    def project(values, readout, heads, j, g):
        first = jnp.bitwise_xor(me, j) % near * heads + g
        cols = pl.ds(pl.multiple_of(first * DH, DH), 2 * DH)
        pair = readout[:, cols]
        none = jnp.zeros((readout.shape[0], DH), BF16)
        left = jnp.concatenate([pair[:, :DH], none], axis=1)
        right = jnp.concatenate([none, pair[:, DH:]], axis=1)
        both = jnp.concatenate([left, right], axis=0)
        out = lax.dot_general(values[:, cols], both, NT, preferred_element_type=F32)
        return out.astype(BF16)

    copies[0].wait()
    copies[1].wait()
    for j in range(near):
        put(j, rows["svr"], project(sv, sr, small_group, j, 0))
    copies[2].wait()
    copies[3].wait()
    for j in range(near):
        for g in range(0, group, 2):
            put(j, rows["vr"] + g // 2 * tokens, project(bv, br, group, j, g))
    copies[4].wait()
    copies[5].wait()
    for j in range(near):
        for g in range(small_group):
            cols = columns(j, small_group, g)
            put(j, rows["sk"] + g * small_tokens, sk[:, cols])
            outs[j][pl.ds(rows["sq"] + g * small_tokens, small_tokens), :] = sq[:, cols]
    copies[6].wait()
    copies[7].wait()
    for j in range(near):
        for g in range(group):
            cols = columns(j, group, g)
            put(j, rows["k"] + g * tokens, bk[:, cols])
            outs[j][pl.ds(rows["q"] + g * tokens, tokens), :] = bq[:, cols]


def gather_small_kernel(order, near, rows, *refs):
    n = len(order)
    blocks, (guidance, out, weight) = refs[:n], refs[n:]
    weight[:, :] = jnp.full(weight.shape, guidance[0], F32)
    at = 0
    for block, k in zip(blocks, order):
        parts = [(rows["sk"], rows["far"])] + ([(rows["sq"], rows["near"])] if k < near else [])
        for first, last in parts:
            out[pl.ds(at, last - first), :] = block[pl.ds(first, last - first), :]
            at += last - first


def attend_heads(heads, lat):
    scale = math.log2(math.e) / math.sqrt(DH)
    scores = [
        lax.dot_general(keys, queries, NT, preferred_element_type=F32)
        for queries, keys, _ in heads
    ]
    weights, totals = [], []
    for x in scores:
        probs = jnp.exp2((x - jnp.max(x, axis=0, keepdims=True)) * scale)
        totals.append(jnp.sum(probs, axis=0, keepdims=True))
        weights.append(probs.astype(BF16))
    out = None
    for (_, _, values), weight, total in zip(heads, weights, totals):
        part = jnp.dot(values, weight, preferred_element_type=F32) / total
        out = part if out is None else out + part
    return out


def big_kernel(order, near, group, tokens, lat, rows, *refs):
    n = len(order)
    blocks, out = refs[:n], refs[n]
    here = [b for b, k in zip(blocks, order) if k < near]
    read = lambda some, first: jnp.concatenate(
        [b[pl.ds(first, tokens), :] for b in some], axis=0
    )
    values = [read(blocks, rows["vr"] + p * tokens).T for p in range(group // 2)]
    out[:, :] = attend_heads(
        [
            (
                read(here, rows["q"] + g * tokens),
                read(blocks, rows["k"] + g * tokens),
                values[g // 2][g % 2 * lat : (g % 2 + 1) * lat, :],
            )
            for g in range(group)
        ],
        lat,
    )


def small_kernel(order, near, small_group, tokens, count, lat, rows, *refs):
    n = len(order)
    blocks, theirs, out = refs[:n], refs[n], refs[n + 1]
    first_core = lax.axis_index("head") == 0
    at = 0
    found = {name: [] for name in ("sk", "svr", "sq")}
    for block, k in zip(blocks, order):
        for name, size in (
            ("sk", small_group * count),
            ("svr", count),
            ("sq", small_group * count),
        ):
            if name == "sq" and k >= near:
                continue
            own = block[pl.ds(rows[name], size), :]
            found[name].append((own, theirs[pl.ds(at, size), :]))
            at += size
    values = jnp.concatenate([p[side] for side in (0, 1) for p in found["svr"]], axis=0).T
    heads = []
    for g in range(small_group):
        head = slice(g * count, (g + 1) * count)
        keys = [p[side][head] for side in (0, 1) for p in found["sk"]]
        queries = []
        for own, other in found["sq"]:
            queries.append(jnp.where(first_core, own[head], other[head]))
            queries.append(jnp.where(first_core, other[head], own[head]))
        heads.append(
            (
                jnp.concatenate(queries, axis=0),
                jnp.concatenate(keys, axis=0),
                values[g * lat : (g + 1) * lat, :],
            )
        )
    out[:, :] = attend_heads(heads, lat)


def blend_kernel(near, tokens, big, other_big, small, weight, *refs):
    outs, latent = refs[:near], refs[near]
    lat, width = big.shape
    scale = weight[:1, :1]
    blended = (1.0 + scale) * (big[:, :] + other_big[:, :]) - scale * small[:, :]
    latent[:width, :lat] = blended.T
    for i in range(near):
        even = latent[pl.ds(i * tokens, tokens // 2, stride=2), :lat]
        odd = latent[pl.ds(i * tokens + 1, tokens // 2, stride=2), :lat]
        outs[i][:, :] = jnp.concatenate([even, odd], axis=1)


def sum_kernel(*refs):
    total = refs[0][:, :]
    for x in refs[1:-1]:
        total = total + x[:, :]
    refs[-1][:, :] = total


def call(kernel, out_shape, operands, specs=None, scratch=(), cost=None):
    single = not isinstance(out_shape, (list, tuple))
    return pl.pallas_call(
        kernel,
        out_shape=out_shape,
        in_specs=specs if specs is not None else [VMEM] * len(operands),
        out_specs=VMEM if single else [VMEM] * len(out_shape),
        scratch_shapes=list(scratch),
        cost_estimate=cost,
        compiler_params=pltpu.CompilerParams(vmem_limit_bytes=16 * 2**20),
    )(*operands)


def exchange_shards(bq, bk, bv, sq, sk, sv, br, sr, guidance):
    n, cores = lax.axis_size("seq"), lax.axis_size("head")
    near = near_count(n)
    order = hop_order(n)
    tokens, count = bq.shape[0], sq.shape[0]
    group, small_group = bq.shape[1] // DH // near, sq.shape[1] // DH // near
    lat = br.shape[1]
    rows = row_layout(group, small_group, tokens, count)
    shape = lambda *dims, dtype=BF16: jax.ShapeDtypeStruct(dims, dtype)
    sources = [
        pltpu.with_memory_space_constraint(a, pltpu.HBM)
        for a in (sv, sr.T, bv, br.T, sk, sq, bk, bq)
    ]
    sent = call(
        functools.partial(pack_kernel, n, near, group, small_group, rows),
        [shape(rows["near" if k < near else "far"], DH) for k in range(n)],
        sources,
        specs=[HBM] * len(sources),
        scratch=[pltpu.VMEM(a.shape, a.dtype) for a in sources]
        + [pltpu.SemaphoreType.DMA((len(sources),))],
    )
    blocks = [sent[0]]
    for k in order[1:]:
        blocks.append(lax.ppermute(sent[k], "seq", [(j, j ^ k) for j in range(n)]))
    ours, weight = call(
        functools.partial(gather_small_kernel, order, near, rows),
        [
            shape(n * (rows["far"] - rows["sk"]) + near * (rows["near"] - rows["sq"]), DH),
            shape(8, DH, dtype=F32),
        ],
        (*blocks, guidance),
        specs=[VMEM] * n + [SMEM],
    )
    swap = lambda a: lax.ppermute(a, "head", [(c, c ^ 1) for c in range(cores)])
    theirs = swap(ours)
    big = call(
        functools.partial(big_kernel, order, near, group, tokens, lat, rows),
        shape(lat, near * tokens, dtype=F32),
        blocks,
        cost=pl.CostEstimate(flops=10**9, bytes_accessed=10**6, transcendentals=10**5),
    )
    other_big = swap(big)
    small = call(
        functools.partial(small_kernel, order, near, small_group, tokens, count, lat, rows),
        shape(lat, near * tokens, dtype=F32),
        (*blocks, theirs),
        cost=pl.CostEstimate(flops=10**9, bytes_accessed=10**6, transcendentals=10**5),
    )
    hops = [k for k in order if k < near]
    terms = call(
        functools.partial(blend_kernel, near, tokens),
        [shape(tokens // 2, 2 * lat, dtype=F32)] * near,
        (big, other_big, small, weight),
        scratch=[pltpu.VMEM((near * tokens + 8, DH), F32)],
    )
    sums = [terms[0]]
    for i in (3, 2, 1):
        pairs = [(j * cores + c, (j ^ hops[i]) * cores + (c ^ 1)) for j in range(n) for c in range(cores)]
        sums.append(lax.ppermute(terms[i], ("seq", "head"), pairs))
    return call(sum_kernel, shape(tokens // 2, 2 * lat, dtype=F32), sums)


def fits_exchange(mesh, bq, sq, br):
    groups, n, cores = mesh.shape["groups"], mesh.shape["seq"], mesh.shape["head"]
    near = near_count(n)
    tokens = bq.shape[0] // (groups * n)
    count = sq.shape[0] // (groups * n * cores)
    big_heads, small_heads = bq.shape[1] // DH // cores, sq.shape[1] // DH
    return (
        cores == 2
        and n & (n - 1) == 0
        and near >= 1
        and small_heads == near * cores
        and big_heads % (2 * near) == 0
        and 2 * br.shape[1] == DH
        and count % 16 == 0
        and n * tokens <= 1024
    )


def split_heads(matrix, blocks, parts):
    rows_here, columns = matrix.shape
    shaped = matrix.reshape(blocks, rows_here // blocks, parts, columns // parts)
    shaped = jnp.transpose(shaped, (0, 2, 1, 3))
    return shaped.reshape(blocks * parts, rows_here // blocks, columns // parts)


def copy_heads(matrix, blocks, parts):
    rows_here, columns = matrix.shape
    shaped = jnp.transpose(matrix.reshape(rows_here, parts, columns // parts), (1, 0, 2))
    shaped = jnp.broadcast_to(shaped[None], (blocks, parts, rows_here, columns // parts))
    return shaped.reshape(blocks * parts, rows_here, columns // parts)


def join_heads(stacked, blocks, parts):
    pieces, rows_here, columns = stacked.shape
    shaped = stacked.reshape(blocks, parts, rows_here, columns)
    shaped = jnp.transpose(shaped, (0, 2, 1, 3))
    return shaped.reshape(blocks * rows_here, parts * columns)


def attend(query_rows, key_rows, value_rows):
    query_count = query_rows.shape[0]
    heads_here = query_rows.shape[1] // DH
    key_count = key_rows.shape[0]
    block_height = math.gcd(query_count, 256)
    block_count = query_count // block_height
    query_blocks = query_rows.reshape(block_count, block_height, heads_here, DH)
    key_split = key_rows.reshape(key_count, heads_here, DH)
    value_split = value_rows.reshape(key_count, heads_here, DH)
    score_scale = 1.0 / math.sqrt(DH)

    def one_block(query_block):
        scores = (
            jnp.einsum("qgd,kgd->gqk", query_block, key_split, preferred_element_type=F32)
            * score_scale
        )
        row_max = jnp.max(scores, axis=2, keepdims=True)
        probs = jnp.exp(scores - row_max)
        totals = jnp.sum(probs, axis=2, keepdims=True)
        weights = probs.astype(BF16)
        accumulated = jnp.einsum(
            "gqk,kgd->gqd", weights, value_split, preferred_element_type=F32
        )
        attended = accumulated / totals
        attended = jnp.transpose(attended, (1, 0, 2)).reshape(block_height, heads_here * DH)
        return attended.astype(BF16)

    outputs = lax.map(one_block, query_blocks)
    return outputs.reshape(query_count, heads_here * DH)


def seq_exchange(stacked, split, concat):
    return lax.all_to_all(stacked, "seq", split_axis=split, concat_axis=concat, tiled=True)


def run_model(queries, keys, values, shared):
    seq_count = lax.axis_size("seq")
    heads = queries.shape[1] // DH
    blocks = max(seq_count // heads, 1)
    parts = heads // max(heads // seq_count, 1)
    query_rows = seq_exchange(split_heads(queries, blocks, parts), 0, 1)[0]
    key_rows = seq_exchange(copy_heads(keys, blocks, parts), 0, 1)[0]
    value_rows = seq_exchange(copy_heads(values, blocks, parts), 0, 1)[0]
    if shared:
        key_rows = lax.all_gather(key_rows, "head", axis=0, tiled=True)
        value_rows = lax.all_gather(value_rows, "head", axis=0, tiled=True)
    out = attend(query_rows, key_rows, value_rows)
    return join_heads(seq_exchange(out[None], 1, 0), blocks, parts)


def general_shards(bq, bk, bv, sq, sk, sv, br, sr, guidance):
    big_attention = run_model(bq, bk, bv, False)
    big_partial = jnp.dot(big_attention, br, preferred_element_type=F32)
    small_attention = run_model(sq, sk, sv, True)
    small_latent = jnp.dot(small_attention, sr, preferred_element_type=F32)
    weight_value = guidance[0]
    core_index = lax.axis_index("head")
    placed = lax.dynamic_update_slice(
        jnp.zeros_like(big_partial),
        small_latent,
        (core_index * small_latent.shape[0], jnp.zeros((), jnp.int32)),
    )
    blended = lax.psum((1.0 + weight_value) * big_partial - weight_value * placed, "head")
    return blended.reshape(blended.shape[0] // 2, 2 * blended.shape[1])


def solution(mesh):
    placed = (
        P(("groups", "seq"), "head"),
        P(("groups", "seq"), "head"),
        P(("groups", "seq"), "head"),
        P(("groups", "seq", "head"), None),
        P(("groups", "seq", "head"), None),
        P(("groups", "seq", "head"), None),
        P("head", None),
        P(),
        P("groups"),
    )

    def whole(*arrays):
        fits = fits_exchange(mesh, arrays[0], arrays[3], arrays[6])
        return jax.shard_map(
            exchange_shards if fits else general_shards,
            mesh=mesh,
            in_specs=placed,
            out_specs=P(("groups", "seq"), None),
            check_vma=False,
        )(*arrays)

    return whole
```

```python
import functools
import math

import jax
import jax.numpy as jnp
from jax import lax
from jax.experimental import pallas as pl
from jax.experimental.pallas import tpu as pltpu
from jax.sharding import PartitionSpec as P

DH = 128
BF16 = jnp.bfloat16
F32 = jnp.float32
VMEM = pl.BlockSpec(memory_space=pltpu.VMEM)
HBM = pl.BlockSpec(memory_space=pltpu.HBM)
SMEM = pl.BlockSpec(memory_space=pltpu.SMEM)
NT = (((1,), (1,)), ((), ()))


def near_count(n):
    return n // 2


def hop_order(n):
    return [0] + [6, 2, 5, 3, 7, 4, 1] if n == 8 else list(range(n))


def row_layout(group, small_group, tokens, small_tokens):
    rows = {}
    at = 0
    for name, count in (
        ("k", group * tokens),
        ("vr", group // 2 * tokens),
        ("sk", small_group * small_tokens),
        ("svr", small_tokens),
        ("far", 0),
        ("q", group * tokens),
        ("sq", small_group * small_tokens),
        ("near", 0),
    ):
        rows[name] = at
        at += count
    return rows


def pack_kernel(n, near, group, small_group, rows, *refs):
    sources, outs, held, done = refs[:8], refs[8 : 8 + n], refs[8 + n : 16 + n], refs[16 + n]
    copies = [pltpu.make_async_copy(sources[i], held[i], done.at[i]) for i in range(8)]
    for copy in copies:
        copy.start()
    sv, sr, bv, br, sk, sq, bk, bq = held
    tokens, small_tokens = bk.shape[0], sk.shape[0]
    me = lax.axis_index("seq")

    def columns(j, heads, g):
        first = jnp.bitwise_xor(me, j) % near * heads + g
        return pl.ds(pl.multiple_of(first * DH, DH), DH)

    def put(j, row, value):
        for k in range(j, n, near):
            outs[k][pl.ds(row, value.shape[0]), :] = value

    def project(values, readout, heads, j, g):
        first = jnp.bitwise_xor(me, j) % near * heads + g
        cols = pl.ds(pl.multiple_of(first * DH, DH), 2 * DH)
        pair = readout[:, cols]
        none = jnp.zeros((readout.shape[0], DH), BF16)
        left = jnp.concatenate([pair[:, :DH], none], axis=1)
        right = jnp.concatenate([none, pair[:, DH:]], axis=1)
        both = jnp.concatenate([left, right], axis=0)
        out = lax.dot_general(values[:, cols], both, NT, preferred_element_type=F32)
        return out.astype(BF16)

    copies[0].wait()
    copies[1].wait()
    for j in range(near):
        put(j, rows["svr"], project(sv, sr, small_group, j, 0))
    copies[4].wait()
    copies[5].wait()
    for j in range(near):
        for g in range(small_group):
            cols = columns(j, small_group, g)
            put(j, rows["sk"] + g * small_tokens, sk[:, cols])
            outs[j][pl.ds(rows["sq"] + g * small_tokens, small_tokens), :] = sq[:, cols]
    copies[2].wait()
    copies[3].wait()
    for j in range(near):
        for g in range(0, group, 2):
            put(j, rows["vr"] + g // 2 * tokens, project(bv, br, group, j, g))
    copies[6].wait()
    copies[7].wait()
    for j in range(near):
        for g in range(group):
            cols = columns(j, group, g)
            put(j, rows["k"] + g * tokens, bk[:, cols])
            outs[j][pl.ds(rows["q"] + g * tokens, tokens), :] = bq[:, cols]


def gather_small_kernel(order, near, rows, *refs):
    n = len(order)
    blocks, (guidance, out, weight) = refs[:n], refs[n:]
    weight[:, :] = jnp.full(weight.shape, guidance[0], F32)
    at = 0
    for block, k in zip(blocks, order):
        parts = [(rows["sk"], rows["far"])] + ([(rows["sq"], rows["near"])] if k < near else [])
        for first, last in parts:
            out[pl.ds(at, last - first), :] = block[pl.ds(first, last - first), :]
            at += last - first


def attend_heads(heads, lat):
    scale = math.log2(math.e) / math.sqrt(DH)
    scores = [
        lax.dot_general(keys, queries, NT, preferred_element_type=F32)
        for queries, keys, _ in heads
    ]
    weights, totals = [], []
    for x in scores:
        probs = jnp.exp2((x - jnp.max(x, axis=0, keepdims=True)) * scale)
        totals.append(jnp.sum(probs, axis=0, keepdims=True))
        weights.append(probs.astype(BF16))
    out = None
    for (_, _, values), weight, total in zip(heads, weights, totals):
        part = jnp.dot(values, weight, preferred_element_type=F32) / total
        out = part if out is None else out + part
    return out


def big_kernel(order, near, group, tokens, lat, rows, *refs):
    n = len(order)
    blocks, out = refs[:n], refs[n]
    here = [b for b, k in zip(blocks, order) if k < near]
    read = lambda some, first: jnp.concatenate(
        [b[pl.ds(first, tokens), :] for b in some], axis=0
    )
    values = [read(blocks, rows["vr"] + p * tokens).T for p in range(group // 2)]
    out[:, :] = attend_heads(
        [
            (
                read(here, rows["q"] + g * tokens),
                read(blocks, rows["k"] + g * tokens),
                values[g // 2][g % 2 * lat : (g % 2 + 1) * lat, :],
            )
            for g in range(group)
        ],
        lat,
    )


def small_kernel(order, near, small_group, tokens, count, lat, rows, *refs):
    n = len(order)
    blocks, theirs, out = refs[:n], refs[n], refs[n + 1]
    first_core = lax.axis_index("head") == 0
    at = 0
    found = {name: [] for name in ("sk", "svr", "sq")}
    for block, k in zip(blocks, order):
        for name, size in (
            ("sk", small_group * count),
            ("svr", count),
            ("sq", small_group * count),
        ):
            if name == "sq" and k >= near:
                continue
            own = block[pl.ds(rows[name], size), :]
            found[name].append((own, theirs[pl.ds(at, size), :]))
            at += size
    values = jnp.concatenate([p[side] for side in (0, 1) for p in found["svr"]], axis=0).T
    heads = []
    for g in range(small_group):
        head = slice(g * count, (g + 1) * count)
        keys = [p[side][head] for side in (0, 1) for p in found["sk"]]
        queries = []
        for own, other in found["sq"]:
            queries.append(jnp.where(first_core, own[head], other[head]))
            queries.append(jnp.where(first_core, other[head], own[head]))
        heads.append(
            (
                jnp.concatenate(queries, axis=0),
                jnp.concatenate(keys, axis=0),
                values[g * lat : (g + 1) * lat, :],
            )
        )
    out[:, :] = attend_heads(heads, lat)


def blend_kernel(near, tokens, big, other_big, small, weight, *refs):
    outs, latent = refs[:near], refs[near]
    lat, width = big.shape
    scale = weight[:1, :1]
    blended = (1.0 + scale) * (big[:, :] + other_big[:, :]) - scale * small[:, :]
    latent[:width, :lat] = blended.T
    for i in range(near):
        even = latent[pl.ds(i * tokens, tokens // 2, stride=2), :lat]
        odd = latent[pl.ds(i * tokens + 1, tokens // 2, stride=2), :lat]
        outs[i][:, :] = jnp.concatenate([even, odd], axis=1)


def sum_kernel(*refs):
    total = refs[0][:, :]
    for x in refs[1:-1]:
        total = total + x[:, :]
    refs[-1][:, :] = total


def call(kernel, out_shape, operands, specs=None, scratch=(), cost=None):
    single = not isinstance(out_shape, (list, tuple))
    return pl.pallas_call(
        kernel,
        out_shape=out_shape,
        in_specs=specs if specs is not None else [VMEM] * len(operands),
        out_specs=VMEM if single else [VMEM] * len(out_shape),
        scratch_shapes=list(scratch),
        cost_estimate=cost,
        compiler_params=pltpu.CompilerParams(vmem_limit_bytes=16 * 2**20),
    )(*operands)


def exchange_shards(bq, bk, bv, sq, sk, sv, br, sr, guidance):
    n, cores = lax.axis_size("seq"), lax.axis_size("head")
    near = near_count(n)
    order = hop_order(n)
    tokens, count = bq.shape[0], sq.shape[0]
    group, small_group = bq.shape[1] // DH // near, sq.shape[1] // DH // near
    lat = br.shape[1]
    rows = row_layout(group, small_group, tokens, count)
    shape = lambda *dims, dtype=BF16: jax.ShapeDtypeStruct(dims, dtype)
    sources = [
        pltpu.with_memory_space_constraint(a, pltpu.HBM)
        for a in (sv, sr.T, bv, br.T, sk, sq, bk, bq)
    ]
    sent = call(
        functools.partial(pack_kernel, n, near, group, small_group, rows),
        [shape(rows["near" if k < near else "far"], DH) for k in range(n)],
        sources,
        specs=[HBM] * len(sources),
        scratch=[pltpu.VMEM(a.shape, a.dtype) for a in sources]
        + [pltpu.SemaphoreType.DMA((len(sources),))],
    )
    blocks = [sent[0]]
    for k in order[1:]:
        blocks.append(lax.ppermute(sent[k], "seq", [(j, j ^ k) for j in range(n)]))
    ours, weight = call(
        functools.partial(gather_small_kernel, order, near, rows),
        [
            shape(n * (rows["far"] - rows["sk"]) + near * (rows["near"] - rows["sq"]), DH),
            shape(8, DH, dtype=F32),
        ],
        (*blocks, guidance),
        specs=[VMEM] * n + [SMEM],
    )
    swap = lambda a: lax.ppermute(a, "head", [(c, c ^ 1) for c in range(cores)])
    theirs = swap(ours)
    big = call(
        functools.partial(big_kernel, order, near, group, tokens, lat, rows),
        shape(lat, near * tokens, dtype=F32),
        blocks,
        cost=pl.CostEstimate(flops=10**9, bytes_accessed=10**6, transcendentals=10**5),
    )
    other_big = swap(big)
    small = call(
        functools.partial(small_kernel, order, near, small_group, tokens, count, lat, rows),
        shape(lat, near * tokens, dtype=F32),
        (*blocks, theirs),
        cost=pl.CostEstimate(flops=10**9, bytes_accessed=10**6, transcendentals=10**5),
    )
    hops = [k for k in order if k < near]
    terms = call(
        functools.partial(blend_kernel, near, tokens),
        [shape(tokens // 2, 2 * lat, dtype=F32)] * near,
        (big, other_big, small, weight),
        scratch=[pltpu.VMEM((near * tokens + 8, DH), F32)],
    )
    sums = [terms[0]]
    for i in (3, 2, 1):
        pairs = [(j * cores + c, (j ^ hops[i]) * cores + (c ^ 1)) for j in range(n) for c in range(cores)]
        sums.append(lax.ppermute(terms[i], ("seq", "head"), pairs))
    return call(sum_kernel, shape(tokens // 2, 2 * lat, dtype=F32), sums)


def fits_exchange(mesh, bq, sq, br):
    groups, n, cores = mesh.shape["groups"], mesh.shape["seq"], mesh.shape["head"]
    near = near_count(n)
    tokens = bq.shape[0] // (groups * n)
    count = sq.shape[0] // (groups * n * cores)
    big_heads, small_heads = bq.shape[1] // DH // cores, sq.shape[1] // DH
    return (
        cores == 2
        and n & (n - 1) == 0
        and near >= 1
        and small_heads == near * cores
        and big_heads % (2 * near) == 0
        and 2 * br.shape[1] == DH
        and count % 16 == 0
        and n * tokens <= 1024
    )


def split_heads(matrix, blocks, parts):
    rows_here, columns = matrix.shape
    shaped = matrix.reshape(blocks, rows_here // blocks, parts, columns // parts)
    shaped = jnp.transpose(shaped, (0, 2, 1, 3))
    return shaped.reshape(blocks * parts, rows_here // blocks, columns // parts)


def copy_heads(matrix, blocks, parts):
    rows_here, columns = matrix.shape
    shaped = jnp.transpose(matrix.reshape(rows_here, parts, columns // parts), (1, 0, 2))
    shaped = jnp.broadcast_to(shaped[None], (blocks, parts, rows_here, columns // parts))
    return shaped.reshape(blocks * parts, rows_here, columns // parts)


def join_heads(stacked, blocks, parts):
    pieces, rows_here, columns = stacked.shape
    shaped = stacked.reshape(blocks, parts, rows_here, columns)
    shaped = jnp.transpose(shaped, (0, 2, 1, 3))
    return shaped.reshape(blocks * rows_here, parts * columns)


def attend(query_rows, key_rows, value_rows):
    query_count = query_rows.shape[0]
    heads_here = query_rows.shape[1] // DH
    key_count = key_rows.shape[0]
    block_height = math.gcd(query_count, 256)
    block_count = query_count // block_height
    query_blocks = query_rows.reshape(block_count, block_height, heads_here, DH)
    key_split = key_rows.reshape(key_count, heads_here, DH)
    value_split = value_rows.reshape(key_count, heads_here, DH)
    score_scale = 1.0 / math.sqrt(DH)

    def one_block(query_block):
        scores = (
            jnp.einsum("qgd,kgd->gqk", query_block, key_split, preferred_element_type=F32)
            * score_scale
        )
        row_max = jnp.max(scores, axis=2, keepdims=True)
        probs = jnp.exp(scores - row_max)
        totals = jnp.sum(probs, axis=2, keepdims=True)
        weights = probs.astype(BF16)
        accumulated = jnp.einsum(
            "gqk,kgd->gqd", weights, value_split, preferred_element_type=F32
        )
        attended = accumulated / totals
        attended = jnp.transpose(attended, (1, 0, 2)).reshape(block_height, heads_here * DH)
        return attended.astype(BF16)

    outputs = lax.map(one_block, query_blocks)
    return outputs.reshape(query_count, heads_here * DH)


def seq_exchange(stacked, split, concat):
    return lax.all_to_all(stacked, "seq", split_axis=split, concat_axis=concat, tiled=True)


def run_model(queries, keys, values, shared):
    seq_count = lax.axis_size("seq")
    heads = queries.shape[1] // DH
    blocks = max(seq_count // heads, 1)
    parts = heads // max(heads // seq_count, 1)
    query_rows = seq_exchange(split_heads(queries, blocks, parts), 0, 1)[0]
    key_rows = seq_exchange(copy_heads(keys, blocks, parts), 0, 1)[0]
    value_rows = seq_exchange(copy_heads(values, blocks, parts), 0, 1)[0]
    if shared:
        key_rows = lax.all_gather(key_rows, "head", axis=0, tiled=True)
        value_rows = lax.all_gather(value_rows, "head", axis=0, tiled=True)
    out = attend(query_rows, key_rows, value_rows)
    return join_heads(seq_exchange(out[None], 1, 0), blocks, parts)


def general_shards(bq, bk, bv, sq, sk, sv, br, sr, guidance):
    big_attention = run_model(bq, bk, bv, False)
    big_partial = jnp.dot(big_attention, br, preferred_element_type=F32)
    small_attention = run_model(sq, sk, sv, True)
    small_latent = jnp.dot(small_attention, sr, preferred_element_type=F32)
    weight_value = guidance[0]
    core_index = lax.axis_index("head")
    placed = lax.dynamic_update_slice(
        jnp.zeros_like(big_partial),
        small_latent,
        (core_index * small_latent.shape[0], jnp.zeros((), jnp.int32)),
    )
    blended = lax.psum((1.0 + weight_value) * big_partial - weight_value * placed, "head")
    return blended.reshape(blended.shape[0] // 2, 2 * blended.shape[1])


def solution(mesh):
    placed = (
        P(("groups", "seq"), "head"),
        P(("groups", "seq"), "head"),
        P(("groups", "seq"), "head"),
        P(("groups", "seq", "head"), None),
        P(("groups", "seq", "head"), None),
        P(("groups", "seq", "head"), None),
        P("head", None),
        P(),
        P("groups"),
    )

    def whole(*arrays):
        fits = fits_exchange(mesh, arrays[0], arrays[3], arrays[6])
        return jax.shard_map(
            exchange_shards if fits else general_shards,
            mesh=mesh,
            in_specs=placed,
            out_specs=P(("groups", "seq"), None),
            check_vma=False,
        )(*arrays)

    return whole
```
